512 devices in a mesh: agent: 16 (over x, y), dp: 32 (over z, core).
Axes of the slice: x: 4, y: 4, z: 16, core: 2. Of those that a mesh axis runs over, the one named last changes fastest.
Arguments:
- learn_obs: bfloat16 [16, 1024, 16, 3456], P('agent', 'dp'), may hold values from -6 to 6
- own_obs: bfloat16 [16, 1024, 3456], P('agent', 'dp'), may hold values from -6 to 6
- opp_obs: bfloat16 [16, 1024, 3456], P('agent', 'dp'), may hold values from -6 to 6
- opponent: int32 [16, 1024, 1], P('agent', 'dp'), may hold values from 0 to 15; in each aligned block of 32 rows (0 to 31, 32 to 63, ..., all dimensions but the last counted through in order) at most 8 rows name the same one
- actions: int32 [16, 1024, 16], P('agent', 'dp'), may hold values from 0 to 17
- done: int32 [16, 1024, 16], P('agent', 'dp'), may hold values 0 or 1
- rewards: float32 [16, 1024, 16], P('agent', 'dp'), may hold values from -6 to 6
- behaviour: float32 [16, 1024, 16], P('agent', 'dp'), may hold values from -4.5 to -1.5
- core_master: float32 [16, 256, 3712], P('agent', 'dp'), may hold values from -0.109375 to 0.109375
- core_mom: float32 [16, 256, 3712], P('agent', 'dp'), may hold values from -6 to 6
- core_vel: float32 [16, 256, 3712], P('agent', 'dp'), may hold values from 0.1 to 1
- head_master: float32 [16, 19, 256], P('agent'), may hold values from -0.375 to 0.375
- head_mom: float32 [16, 19, 256], P('agent'), may hold values from -6 to 6
- head_vel: float32 [16, 19, 256], P('agent'), may hold values from 0.1 to 1
- rates: float32 [16], P('agent'), may hold values from 0.01 to 0.1
Outputs:
- own_logits: float32 [16, 1024, 18], P('agent', 'dp')
- opp_logits: bfloat16 [16, 1024, 18], P('agent', 'dp')
- new_core: float32 [16, 256, 3712], P('agent', 'dp')
- new_core_mom: float32 [16, 256, 3712], P('agent', 'dp')
- new_core_vel: float32 [16, 256, 3712], P('agent', 'dp')
- new_head: float32 [16, 19, 256], P('agent')
- new_head_mom: float32 [16, 19, 256], P('agent')
- new_head_vel: float32 [16, 19, 256], P('agent')
The draws below stay inside these ranges and needn't reach their ends.
Inputs may be any that keep to these rules, and one draw needn't show every extreme that they name: Among the 32 environments of one device (aligned blocks of the environment dimension), at most 8 face the same opponent agent, and some device reaches 8 in every draw.
All inputs are finite; a program needn't handle non-finite values. No bound on the sum of `done` on one device may be relied on, other than what follows from the above.
Results may differ from the reference program's by a relative error of at most 0.023.
Values may be sent and summed in bfloat16 or wider, within the bound.
A program may use at most 64 MiB of HBM per device.

```python
import math
import jax
import jax.numpy as jnp
import numpy as np
from jax import lax

FEAT = 3456
HID = 256
ACTIONS = 18
ENVS_DEV = 32
UNROLL = 16
AGENTS = 16
ENVS = 1024
MOST = 8
HEADS = 19


def touch_ends(array, key, least, top_value):
    shape = array.shape
    index_at = [jax.random.randint(jax.random.fold_in(key, axis), (), 0, shape[axis]) for axis in range(len(shape))]
    array = array.at[tuple(index_at)].set(least)
    longest = shape.index(max(shape))
    index_at[longest] = (index_at[longest] + 1) % shape[longest]
    return array.at[tuple(index_at)].set(top_value)


def block_levels(key, dims, cuts, low, top_value):
    loudness, own = 1.0, jax.random.fold_in(key, 6)
    for dim, parts in cuts:
        steps = jnp.exp(jax.random.uniform(jax.random.fold_in(own, dim), (parts,), jnp.float32, low / len(cuts), top_value / len(cuts)))
        loudness = loudness * jnp.repeat(steps, dims[dim] // parts).reshape([-1 if axis == dim else 1 for axis in range(len(dims))])
    return loudness


def assign_block(key, own, number, rows, amount, top, reach, slope):
    order = jax.random.permutation(key, amount)
    packed, common = shares(amount, rows * top, reach, slope, True), shares(amount, rows * top, reach, slope, False)
    places = jnp.arange(amount)

    def named(tallies, offset_by):
        used = int((tallies > 0).sum())
        fixed = max(1, used // 4)
        shifted = fixed + (places - fixed + offset_by * (used - fixed)) % max(1, amount - fixed)
        return jnp.zeros((amount,), jnp.int32).at[order[jnp.where(places < fixed, places, shifted)]].set(jnp.asarray(tallies, jnp.int32))

    tallies = jnp.where(number % 4 == 0, named(packed, number // 4), named(common, number - number // 4 - 1))
    mixed = jax.random.permutation(jax.random.fold_in(own, 3), amount)
    giver, taker = mixed[0:amount // 2 * 2:2], mixed[1:amount // 2 * 2:2]
    margin = jnp.minimum(tallies[giver] - 1, reach - tallies[taker]) // 2
    margin = jnp.where((giver == order[0]) | (taker == order[0]) | (tallies[taker] == 0), 0, jnp.maximum(margin, 0))
    shifted = jax.random.randint(jax.random.fold_in(own, 4), (amount // 2,), 0, 1 << 20) % (margin + 1)
    tallies = tallies.at[giver].add(-shifted).at[taker].add(shifted)
    items = jnp.searchsorted(jnp.cumsum(tallies), jnp.arange(rows * top), side="right").astype(jnp.int32)
    table = items.reshape(top, rows).T
    table = table[jax.random.permutation(jax.random.fold_in(own, 1), rows)]
    offset_by = jax.random.randint(jax.random.fold_in(own, 2), (rows, 1), 0, top)
    return jnp.take_along_axis(table, (jnp.arange(top)[None, :] + offset_by) % top, axis=1)


def shares(number_of, total, most, skew, full):
    weights = [(1 << 20) // math.isqrt(rank ** skew) + 1 for rank in range(1, number_of + 1)]
    largest = most if full else min(most, max(-(-total // number_of), total * weights[0] // sum(weights)))
    least = 1 if total - largest >= number_of - 1 else 0
    holding, rest = [largest] + [least] * (number_of - 1), total - largest - least * (number_of - 1)
    while rest > 0:
        free = [i for i in range(1, number_of) if holding[i] < largest] or [i for i in range(1, number_of) if holding[i] < most]
        whole, remaining = sum([weights[i] for i in free]), rest
        for i in free:
            more = min(most - holding[i], max(1, remaining * weights[i] // whole), rest)
            holding[i] = holding[i] + more
            rest = rest - more
    return np.array(holding)


def gaussian(own_key, dims, scale, most, cuts=(), kind=jnp.bfloat16):
    loudness = block_levels(own_key, dims, cuts, -0.22, 0.18) if cuts else 1.0
    values = jax.random.normal(own_key, dims, jnp.float32) * scale * loudness
    return jnp.minimum(jnp.maximum(values, -most), most).astype(kind)


def setup_inputs(seed: int = 0) -> dict:
    keys = jax.random.split(jax.random.key(seed), 16)
    learn_obs = gaussian(keys[0], (AGENTS, ENVS, UNROLL, FEAT), 1.0, 6.0, ((0, 16), (1, 32)))
    own_obs = gaussian(keys[1], (AGENTS, ENVS, FEAT), 1.0, 6.0, ((0, 16), (1, 32)))
    opp_obs = gaussian(keys[2], (AGENTS, ENVS, FEAT), 1.0, 6.0, ((0, 16), (1, 32)))
    opponent_keys = jax.random.split(jax.random.fold_in(keys[3], 1), AGENTS * ENVS // ENVS_DEV)
    opponent_turns = jax.random.permutation(jax.random.fold_in(keys[3], 3), AGENTS * ENVS // ENVS_DEV)
    opponent = jax.vmap(lambda own, number: assign_block(jax.random.fold_in(keys[3], 2), own, number, ENVS_DEV, AGENTS, 1, MOST, 2))(opponent_keys, opponent_turns).reshape((AGENTS, ENVS, 1))
    actions = touch_ends(jax.random.randint(keys[4], (AGENTS, ENVS, UNROLL), 0, ACTIONS), jax.random.fold_in(keys[4], 1), 0, ACTIONS - 1).astype(jnp.int32)
    done = touch_ends((jax.random.randint(keys[5], (AGENTS, ENVS, UNROLL), 0, 8) < 1).astype(jnp.int32), jax.random.fold_in(keys[5], 1), 0, 1)
    rewards = gaussian(keys[6], (AGENTS, ENVS, UNROLL), 1.0, 6.0, ((0, 16), (1, 32)), jnp.float32)
    behaviour = jnp.clip(-4.5 + 3.0 * jax.random.uniform(keys[7], (AGENTS, ENVS, UNROLL), jnp.float32) ** block_levels(keys[7], (AGENTS, ENVS, UNROLL), ((0, 16), (1, 32)), -0.2, 0.2), -4.5, -1.5)
    core_master = gaussian(keys[8], (AGENTS, HID, FEAT + HID), FEAT ** -0.5, 0.109375, ((0, 16), (1, 32)), jnp.float32)
    core_mom = gaussian(keys[9], (AGENTS, HID, FEAT + HID), 0.5, 6.0, ((0, 16), (1, 32)), jnp.float32)
    core_vel = jnp.clip(jnp.exp(math.log(1.0) - 2.3025851 * jax.random.uniform(keys[10], (AGENTS, HID, FEAT + HID), jnp.float32) ** block_levels(keys[10], (AGENTS, HID, FEAT + HID), ((0, 16), (1, 32)), -0.2, 0.2)), 0.1, 1.0)
    head_master = gaussian(keys[11], (AGENTS, HEADS, HID), HID ** -0.5, 0.375, ((0, 16),), jnp.float32)
    head_mom = gaussian(keys[12], (AGENTS, HEADS, HID), 0.5, 6.0, ((0, 16),), jnp.float32)
    head_vel = jnp.clip(jnp.exp(math.log(1.0) - 2.3025851 * jax.random.uniform(keys[13], (AGENTS, HEADS, HID), jnp.float32) ** block_levels(keys[13], (AGENTS, HEADS, HID), ((0, 16),), -0.2, 0.2)), 0.1, 1.0)
    rates = jnp.clip(jnp.exp(math.log(0.1) - 2.3025851 * jax.random.uniform(keys[14], (AGENTS,), jnp.float32) ** block_levels(keys[14], (AGENTS,), ((0, 16),), -0.2, 0.2)), 0.01, 0.1)
    return dict(learn_obs=learn_obs, own_obs=own_obs, opp_obs=opp_obs, opponent=opponent, actions=actions, done=done, rewards=rewards, behaviour=behaviour, core_master=core_master, core_mom=core_mom, core_vel=core_vel, head_master=head_master, head_mom=head_mom, head_vel=head_vel, rates=rates)


gamma_rate = 0.99
baseline_cost = 0.5
entropy_cost = 0.05
beta_first = 0.9
beta_second = 0.99
adam_eps = 1e-08

def contract(left, right):
    return lax.dot_general(left, right, (((1,), (1,)), ((), ())), preferred_element_type=jnp.float32)

def contract_rows(left, right):
    return lax.dot_general(left, right, (((0,), (0,)), ((), ())), preferred_element_type=jnp.float32)

def forward(inputs, core_bf, head_bf):
    width = inputs.shape[-1]
    pre_one = contract(inputs, core_bf[:, :width])
    first_act = jax.nn.relu(pre_one)
    first_bf = first_act.astype(jnp.bfloat16)
    pre_two = contract(first_bf, core_bf[:, width:])
    second_act = jax.nn.relu(pre_two) + first_act
    second_bf = second_act.astype(jnp.bfloat16)
    network_outputs = contract(second_bf, head_bf)
    return (network_outputs, pre_one, first_bf, pre_two, second_bf)

def importance_trace_gradients(network_outputs, bootstrap_value, actions, done, rewards, behaviour, scale_factor):
    action_count = network_outputs.shape[-1] - 1
    logits = network_outputs[..., :action_count]
    values = network_outputs[..., action_count]
    totals = lax.optimization_barrier(jnp.sum(jnp.exp(logits), -1))
    logp = logits - jnp.log(totals)[..., None]
    probs = jnp.exp(logp)
    chosen = (actions[..., None] == jnp.arange(action_count, dtype=jnp.int32)).astype(jnp.float32)
    logp_act = lax.optimization_barrier(jnp.sum(logp * chosen, -1))
    ratio = jnp.minimum(1.0, jnp.exp(logp_act - behaviour))
    discount = gamma_rate * (1.0 - done.astype(jnp.float32))
    next_values = jnp.concatenate([values[:, 1:], bootstrap_value[:, None]], 1)
    deltas = ratio * (rewards + discount * next_values - values)

    def backstep(carry, item):
        delta, factor = item
        carry = delta + factor * carry
        return (carry, carry)
    start = jnp.zeros((values.shape[0],), jnp.float32)
    final_carry, corrections = lax.scan(backstep, start, (deltas.T, (discount * ratio).T), reverse=True)
    targets = values + corrections.T
    next_targets = jnp.concatenate([targets[:, 1:], bootstrap_value[:, None]], 1)
    advantage = ratio * (rewards + discount * next_targets - values)
    entropy = -lax.optimization_barrier(jnp.sum(probs * logp, -1))
    grad_logits = scale_factor * (-advantage[..., None] * (chosen - probs) + entropy_cost * probs * (logp + entropy[..., None]))
    grad_value = scale_factor * (-baseline_cost * (targets - values))
    return jnp.concatenate([grad_logits, grad_value[..., None]], -1)

def backward(core_bf, head_bf, output_gradient, pre_one, pre_two, second_bf, width):
    grad_bf = output_gradient.astype(jnp.bfloat16)
    head_grad = contract_rows(grad_bf, second_bf)
    grad_second = jnp.dot(grad_bf, head_bf, preferred_element_type=jnp.float32)
    grad_pre_two = jnp.where(pre_two > 0, grad_second, 0.0).astype(jnp.bfloat16)
    grad_first = grad_second + jnp.dot(grad_pre_two, core_bf[:, width:], preferred_element_type=jnp.float32)
    grad_pre_one = jnp.where(pre_one > 0, grad_first, 0.0).astype(jnp.bfloat16)
    return (head_grad, grad_pre_one, grad_pre_two)

def adam_step(master, moment, second, grad, rate):
    moment = beta_first * moment + (1.0 - beta_first) * grad
    second = beta_second * second + (1.0 - beta_second) * grad * grad
    master = master - rate * moment / (jnp.sqrt(second) + adam_eps)
    return (master, moment, second)

def reference(learn_obs, own_obs, opp_obs, opponent, actions, done, rewards, behaviour, core_master, core_mom, core_vel, head_master, head_mom, head_vel, rates):
    agent_count, environment_total, rollout_length, width = learn_obs.shape
    action_count = head_master.shape[1] - 1
    scale_factor = 1.0 / rollout_length
    opp_flat = opp_obs.reshape(agent_count * environment_total, width)
    opp_ids = opponent.reshape(-1).astype(jnp.int32)

    def per_agent(slot_index):
        core_bf = core_master[slot_index].astype(jnp.bfloat16)
        head_bf = head_master[slot_index].astype(jnp.bfloat16)
        own_out = forward(own_obs[slot_index], core_bf, head_bf)[0]
        bootstrap_value = own_out[:, action_count]
        opp_out = forward(opp_flat, core_bf, head_bf)[0][:, :action_count].astype(jnp.bfloat16)
        rows = learn_obs[slot_index].reshape(environment_total * rollout_length, width)
        network_outputs, pre_one, first_bf, pre_two, second_bf = forward(rows, core_bf, head_bf)
        output_gradient = importance_trace_gradients(network_outputs.reshape(environment_total, rollout_length, action_count + 1), bootstrap_value, actions[slot_index], done[slot_index], rewards[slot_index], behaviour[slot_index], scale_factor)
        output_gradient = output_gradient.reshape(environment_total * rollout_length, action_count + 1)
        head_grad, grad_pre_one, grad_pre_two = backward(core_bf, head_bf, output_gradient, pre_one, pre_two, second_bf, width)
        core_grad = jnp.concatenate([contract_rows(grad_pre_one, rows), contract_rows(grad_pre_two, first_bf)], 1)
        rate = rates[slot_index]
        new_core, new_core_mom, new_core_vel = adam_step(core_master[slot_index], core_mom[slot_index], core_vel[slot_index], core_grad, rate)
        new_head, new_head_mom, new_head_vel = adam_step(head_master[slot_index], head_mom[slot_index], head_vel[slot_index], head_grad, rate)
        return (own_out[:, :action_count], opp_out, new_core, new_core_mom, new_core_vel, new_head, new_head_mom, new_head_vel)
    results = lax.map(per_agent, jnp.arange(agent_count, dtype=jnp.int32))
    own_logits = results[0]
    every_opp = results[1]
    picked = every_opp[opp_ids, jnp.arange(agent_count * environment_total, dtype=jnp.int32)]
    opp_logits = picked.reshape(agent_count, environment_total, action_count)
    return (own_logits, opp_logits, results[2], results[3], results[4], results[5], results[6], results[7])
```

```python
import jax
import jax.numpy as jnp
from jax import lax
from jax.sharding import Mesh
from jax.sharding import PartitionSpec as P

BLOCK = 128
DP = ("dp_0", "dp_1")


gamma_rate = 0.99
baseline_cost = 0.5
entropy_cost = 0.05
beta_first = 0.9
beta_second = 0.99
adam_eps = 1e-08


def joined_along(blocks, dim):
    shape = list(blocks.shape[1:])
    shape[dim] *= blocks.shape[0]
    return jnp.moveaxis(blocks, 0, dim).reshape(shape)


def stacked_from(x, axes, order):
    blocks = x[None]
    for k in order:
        blocks = lax.all_gather(blocks, axes[k], axis=0, tiled=True)
    current = [lax.axis_size(axes[k]) for k in reversed(order)]
    blocks = blocks.reshape(*current, *x.shape)
    turned = sorted(range(len(order)), key=lambda place: order[len(order) - 1 - place])
    return blocks.transpose(*turned, *range(len(order), blocks.ndim)).reshape(-1, *x.shape)


def gather_axes(x, axes, order, dim):
    return joined_along(stacked_from(x, axes, order), dim)


def reduced_to_own(blocks, axes, order):
    shape = [lax.axis_size(a) for a in axes]
    blocks = blocks.reshape(*shape, *blocks.shape[1:])
    blocks = blocks.transpose(*order, *range(len(axes), blocks.ndim))
    blocks = blocks.reshape(-1, *blocks.shape[len(axes) :])
    for k in order:
        blocks = lax.psum_scatter(blocks, axes[k], scatter_dimension=0, tiled=True)
    return blocks[0]


def in_blocks(x, dim, peers):
    before, after = (x.shape[:dim], x.shape[dim + 1 :])
    return jnp.moveaxis(x.reshape(*before, peers, -1, *after), dim, 0)


def sum_by_axis(x, axes, order, dim):
    peers = lax.axis_size(axes)
    return reduced_to_own(in_blocks(x, dim, peers), axes, order)


def by_axis(x, axes):
    for axis in axes:
        x = lax.psum(x, axis)
    return x


def contract(left, right):
    return lax.dot_general(
        left, right, (((1,), (1,)), ((), ())), preferred_element_type=jnp.float32
    )


def contract_rows(left, right):
    return lax.dot_general(
        left, right, (((0,), (0,)), ((), ())), preferred_element_type=jnp.float32
    )


def forward(inputs, core_bf, head_bf):
    width = inputs.shape[-1]
    pre_one = contract(inputs, core_bf[:, :width])
    first_act = jax.nn.relu(pre_one)
    first_bf = first_act.astype(jnp.bfloat16)
    pre_two = contract(first_bf, core_bf[:, width:])
    second_act = jax.nn.relu(pre_two) + first_act
    second_bf = second_act.astype(jnp.bfloat16)
    network_outputs = contract(second_bf, head_bf)
    return (network_outputs, pre_one, first_bf, pre_two, second_bf)


def importance_trace_gradients(
    network_outputs, bootstrap_value, actions, done, rewards, behaviour, scale_factor
):
    action_count = network_outputs.shape[-1] - 1
    logits = network_outputs[..., :action_count]
    values = network_outputs[..., action_count]
    totals = jnp.sum(jnp.exp(logits), -1)
    logp = logits - jnp.log(totals)[..., None]
    probs = jnp.exp(logp)
    chosen = (actions[..., None] == jnp.arange(action_count, dtype=jnp.int32)).astype(jnp.float32)
    logp_act = jnp.sum(logp * chosen, -1)
    ratio = jnp.minimum(1.0, jnp.exp(logp_act - behaviour))
    discount = gamma_rate * (1.0 - done.astype(jnp.float32))
    next_values = jnp.concatenate([values[:, 1:], bootstrap_value[:, None]], 1)
    deltas = ratio * (rewards + discount * next_values - values)

    def backstep(carry, item):
        delta, factor = item
        carry = delta + factor * carry
        return (carry, carry)

    start = jnp.zeros((values.shape[0],), jnp.float32)
    final_carry, corrections = lax.scan(
        backstep, start, (deltas.T, (discount * ratio).T), reverse=True
    )
    targets = values + corrections.T
    next_targets = jnp.concatenate([targets[:, 1:], bootstrap_value[:, None]], 1)
    advantage = ratio * (rewards + discount * next_targets - values)
    entropy = -jnp.sum(probs * logp, -1)
    grad_logits = scale_factor * (
        -advantage[..., None] * (chosen - probs)
        + entropy_cost * probs * (logp + entropy[..., None])
    )
    grad_value = scale_factor * (-baseline_cost * (targets - values))
    return jnp.concatenate([grad_logits, grad_value[..., None]], -1)


def adam_step(master, moment, second, grad, rate):
    moment = beta_first * moment + (1.0 - beta_first) * grad
    second = beta_second * second + (1.0 - beta_second) * grad * grad
    master = master - rate * moment / (jnp.sqrt(second) + adam_eps)
    return (master, moment, second)


def per_device(
    learn_obs,
    own_obs,
    opp_obs,
    opponent,
    actions,
    done,
    rewards,
    behaviour,
    core_master,
    core_mom,
    core_vel,
    head_master,
    head_mom,
    head_vel,
    rates,
):
    environment_total, rollout_length, width = (
        learn_obs.shape[1],
        learn_obs.shape[2],
        learn_obs.shape[3],
    )
    action_count = head_master.shape[1] - 1
    agent_count = lax.axis_size("agent")
    slots = min(environment_total, BLOCK // agent_count)
    scale_factor = 1.0 / rollout_length
    core_bf = gather_axes(core_master.astype(jnp.bfloat16), DP, (0, 1), 1)[0]
    head_bf = head_master[0].astype(jnp.bfloat16)
    own_out = forward(own_obs[0], core_bf, head_bf)[0]
    ids = opponent[0, :, 0]
    earlier = (ids[None, :] == ids[:, None]) & jnp.tril(jnp.ones((ids.shape[0],) * 2, bool), -1)
    ranks = jnp.sum(earlier.astype(jnp.int32), 1)
    position = ids * slots + ranks
    placing = (
        position[None, :] == jnp.arange(agent_count * slots, dtype=jnp.int32)[:, None]
    ).astype(jnp.bfloat16)
    outgoing = jnp.dot(placing, opp_obs[0], preferred_element_type=jnp.float32).astype(jnp.bfloat16)
    outgoing = outgoing.reshape(agent_count, slots, width)
    incoming = lax.all_to_all(outgoing, "agent", split_axis=0, concat_axis=0, tiled=True)
    count = incoming.shape[1]
    played = forward(incoming.reshape(agent_count * count, width), core_bf, head_bf)[0][
        :, :action_count
    ]
    played = played.astype(jnp.bfloat16).reshape(agent_count, count, action_count)
    returned = lax.all_to_all(played, "agent", split_axis=0, concat_axis=0, tiled=True)
    opp_logits = returned.reshape(agent_count * slots, action_count)[position]
    rows = learn_obs[0].reshape(environment_total * rollout_length, width)
    network_outputs, pre_one, first_bf, pre_two, second_bf = forward(rows, core_bf, head_bf)
    output_gradient = importance_trace_gradients(
        network_outputs.reshape(environment_total, rollout_length, action_count + 1),
        own_out[:, action_count],
        actions[0],
        done[0],
        rewards[0],
        behaviour[0],
        scale_factor,
    )
    grad_bf = output_gradient.reshape(environment_total * rollout_length, action_count + 1).astype(
        jnp.bfloat16
    )
    head_grad = contract_rows(grad_bf, second_bf)
    grad_second = jnp.dot(grad_bf, head_bf, preferred_element_type=jnp.float32)
    grad_pre_two = jnp.where(pre_two > 0, grad_second, 0.0).astype(jnp.bfloat16)
    grad_first = grad_second + jnp.dot(
        grad_pre_two, core_bf[:, width:], preferred_element_type=jnp.float32
    )
    grad_pre_one = jnp.where(pre_one > 0, grad_first, 0.0).astype(jnp.bfloat16)
    core_grad = sum_by_axis(
        jnp.concatenate(
            [contract_rows(grad_pre_one, rows), contract_rows(grad_pre_two, first_bf)], 1
        ).astype(jnp.bfloat16),
        DP,
        (1, 0),
        0,
    ).astype(jnp.float32)
    head_total = by_axis(head_grad, DP)
    rate = rates[0]
    new_core, new_core_mom, new_core_vel = adam_step(
        core_master[0], core_mom[0], core_vel[0], core_grad, rate
    )
    new_head, new_head_mom, new_head_vel = adam_step(
        head_master[0], head_mom[0], head_vel[0], head_total, rate
    )
    return (
        own_out[:, :action_count][None],
        opp_logits[None],
        new_core[None],
        new_core_mom[None],
        new_core_vel[None],
        new_head[None],
        new_head_mom[None],
        new_head_vel[None],
    )


def solution(mesh):
    torus = Mesh(mesh.devices.reshape(mesh.shape["agent"], 16, 2), ("agent", "dp_0", "dp_1"))
    return jax.shard_map(
        per_device,
        mesh=torus,
        in_specs=(
            P("agent", DP, None, None),
            P("agent", DP, None),
            P("agent", DP, None),
            P("agent", DP, None),
            P("agent", DP, None),
            P("agent", DP, None),
            P("agent", DP, None),
            P("agent", DP, None),
            P("agent", DP, None),
            P("agent", DP, None),
            P("agent", DP, None),
            P("agent", None, None),
            P("agent", None, None),
            P("agent", None, None),
            P("agent"),
        ),
        out_specs=(
            P("agent", DP, None),
            P("agent", DP, None),
            P("agent", DP, None),
            P("agent", DP, None),
            P("agent", DP, None),
            P("agent", None, None),
            P("agent", None, None),
            P("agent", None, None),
        ),
        check_vma=False,
    )
```

```python
import functools

import jax
import jax.numpy as jnp
from jax import lax
from jax.experimental import pallas as pl
from jax.experimental.pallas import tpu as pltpu
from jax.sharding import PartitionSpec as P

MESH = pl.DeviceIdType.MESH
F32 = jnp.float32
BF16 = jnp.bfloat16
SLOTS = 8
PAD = 128
CHUNKS = 4

gamma_rate = 0.99
baseline_cost = 0.5
entropy_cost = 0.05
beta_first = 0.9
beta_second = 0.99
adam_eps = 1e-08


def dot(left, right, dims=((1,), (0,)), precision=None):
    return lax.dot_general(left, right, (dims, ((), ())), precision=precision, preferred_element_type=F32)


def bounds(total, parts, unit=128):
    units = -(-total // unit)
    return [min(total, unit * (units * i // parts)) for i in range(parts + 1)]


def column(row_vector, sublanes):
    return jnp.broadcast_to(row_vector, (sublanes, row_vector.shape[1]))


def trace_gradient(out, boot, actions, done, rewards, behaviour, actions_total, steps):
    rows, frames = out.shape
    scale = 1.0 / steps
    row = lax.broadcasted_iota(jnp.int32, (rows, frames), 0)
    time = lax.broadcasted_iota(jnp.int32, (8, frames), 1) % steps
    is_logit = row < actions_total
    values = column(out[actions_total : actions_total + 1, :], 8)
    total = jnp.sum(jnp.where(is_logit, jnp.exp(out), 0.0), 0, keepdims=True)
    logp = out - jnp.log(total)
    probs = jnp.where(is_logit, jnp.exp(logp), 0.0)
    chosen = (row.astype(F32) == actions).astype(F32)
    logp_act = jnp.sum(jnp.where(is_logit, logp, 0.0) * chosen, 0, keepdims=True)
    entropy = -jnp.sum(probs * jnp.where(is_logit, logp, 0.0), 0, keepdims=True)
    ratio = column(jnp.minimum(1.0, jnp.exp(logp_act - behaviour)), 8)
    discount = column(gamma_rate * (1.0 - done), 8)
    rewards, boot = column(rewards, 8), column(boot, 8)
    last = time == steps - 1

    def later(x, by):
        return pltpu.roll(x, frames - by, 1)

    next_values = jnp.where(last, boot, later(values, 1))
    corr = ratio * (rewards + discount * next_values - values)
    factor = discount * ratio
    by = 1
    while by < steps:
        inside = time < steps - by
        corr, factor = (
            corr + factor * jnp.where(inside, later(corr, by), 0.0),
            factor * jnp.where(inside, later(factor, by), 0.0),
        )
        by *= 2
    targets = values + corr
    next_targets = jnp.where(last, boot, later(targets, 1))
    advantage = ratio * (rewards + discount * next_targets - values)
    grad_logits = scale * (
        -advantage[:1] * (chosen - probs) + entropy_cost * probs * (logp + entropy)
    )
    grad_value = scale * (-baseline_cost * (targets - values))[:1]
    return jnp.where(is_logit, grad_logits, jnp.where(row == actions_total, grad_value, 0.0))


def step_kernel(
    sizes,
    learn_hbm, own_hbm, opp_hbm, opponent_hbm, actions_hbm, done_hbm, rewards_hbm, behaviour_hbm, core_hbm, head_hbm,
    grad_out, head_out, own_out, opp_out,
    x, own, opp, opponent, actions, done, rewards, behaviour, core, head,
    shards, weights, pre, mine, for_sibling, from_sibling, sums_out, sums_in, frames_out, frames_in,
    played_out, played_in, heads, head_part, head_from, head_all, head_final,
    load_sem, gather_send, gather_recv, pair_send, pair_recv, own_send, own_recv,
    frame_send, frame_recv, played_send, played_recv, reduce_send, reduce_recv,
    half_send, half_recv, hring_send, hring_recv, hpair_send, hpair_recv, hlast_send, hlast_recv,
):
    (agents, chips, shard, envs, steps, feat, units, head_rows, agent_y) = sizes
    frames = envs * steps
    width = feat + units
    acts = head_rows - 1
    edges = bounds(width, CHUNKS)
    far = chips // 2
    half = CHUNKS // 2
    agent, dp = lax.axis_index("agent"), lax.axis_index("dp")
    chip, side = dp // 2, dp % 2
    other = 1 - side
    agent_x = agents // agent_y
    ax, ay = agent // agent_y, agent % agent_y

    def chip_at(offset):
        return lax.rem(chip + (offset + 2 * chips), chips)

    sibling = (agent, 2 * chip + other)
    ring = [(agent, 2 * chip_at(1) + side), (agent, 2 * chip_at(-1) + side)]
    sign = [1, -1]
    shifts = [(i, j) for i in range(agent_x) for j in range(agent_y) if (i, j) != (0, 0)]
    to_agent = [lax.rem(ax + i, agent_x) * agent_y + lax.rem(ay + j, agent_y) for i, j in shifts]
    from_agent = [lax.rem(ax + agent_x - i, agent_x) * agent_y + lax.rem(ay + agent_y - j, agent_y) for i, j in shifts]

    barrier = pltpu.get_barrier_semaphore()
    peers = [sibling, *ring, *[(a, dp) for a in to_agent]]
    for peer in peers:
        pl.semaphore_signal(barrier, inc=1, device_id=peer, device_id_type=MESH)

    loads = [
        pltpu.make_async_copy(src, dst, load_sem.at[i])
        for i, (src, dst) in enumerate((
            (core_hbm.at[0], core), (head_hbm.at[0], head), (opponent_hbm.at[0], opponent), (opp_hbm.at[0], opp),
            (learn_hbm.at[0], x), (own_hbm.at[0], own), (actions_hbm.at[0], actions), (done_hbm.at[0], done),
            (rewards_hbm.at[0], rewards), (behaviour_hbm.at[0], behaviour),
        ))
    ]
    for load in loads:
        load.start()

    def cols(f):
        return pl.ds(edges[f], edges[f + 1] - edges[f])

    def remote(src, dst, send, recv, to):
        return pltpu.make_async_remote_copy(
            src_ref=src, dst_ref=dst, send_sem=send, recv_sem=recv, device_id=to, device_id_type=MESH
        )

    def gather_has(way, s, f):
        return s < far - 1 or (f < half) == (way == 0)

    def gather(way, s, f):
        block = shards.at[chip_at(-sign[way] * s), side, :, cols(f)]
        return remote(block, block, gather_send.at[way, s, f], gather_recv.at[way, s, f], ring[way])

    def gathered(way, s, f):
        block = shards.at[chip_at(-sign[way] * (s + 1)), side, :, cols(f)]
        return remote(block, block, gather_send.at[way, s, f], gather_recv.at[way, s, f], ring[way])

    def pair(way, s, f, which):
        block = shards.at[chip_at(-sign[way] * (s + 1)), which, :, cols(f)]
        return remote(block, block, pair_send.at[way, s, f], pair_recv.at[way, s, f], sibling)

    def own_pair(which):
        block = shards.at[chip, which]
        return remote(block, block, own_send, own_recv, sibling)

    loads[0].wait()
    shards[chip, side] = core[...].astype(BF16)
    pl.semaphore_wait(barrier, len(peers))
    for f in range(CHUNKS):
        for way in (0, 1):
            if gather_has(way, 0, f):
                gather(way, 0, f).start()
    own_pair(side).start()

    for load in loads[1:4]:
        load.wait()
    ids = opponent[...]
    agent_lane = lax.broadcasted_iota(jnp.int32, (envs, PAD), 1)
    member = (ids == agent_lane).astype(F32)
    before = (
        lax.broadcasted_iota(jnp.int32, (envs, envs), 1) < lax.broadcasted_iota(jnp.int32, (envs, envs), 0)
    ).astype(F32)
    ranks = jnp.sum(dot(before.astype(BF16), member.astype(BF16)) * member, 1, keepdims=True)
    position = ids * SLOTS + ranks.astype(jnp.int32)
    lane = lax.broadcasted_iota(jnp.int32, (envs, agents * SLOTS), 1)
    placing = (position == lane).astype(F32)
    placed = placing.T.astype(BF16)
    placing = placing.astype(BF16)
    outgoing = dot(placed, opp[...]).reshape(agents, SLOTS, feat).astype(BF16)
    frames_out[...] = outgoing
    frames_in[agent] = frames_out[agent]

    def send_frames(i):
        return remote(
            frames_out.at[to_agent[i]], frames_in.at[agent], frame_send.at[i], frame_recv.at[i], (to_agent[i], dp)
        )

    def frames_come(i):
        return remote(
            frames_out.at[to_agent[i]], frames_in.at[from_agent[i]], frame_send.at[i], frame_recv.at[i], (to_agent[i], dp)
        )

    for i in range(len(shifts)):
        send_frames(i).start()

    heads[...] = jnp.zeros_like(heads)
    heads[0:head_rows, :] = head[...]
    head_bf = heads[...].astype(BF16)
    head_turned = heads[...].T.astype(BF16)
    small = head_bf[:32]

    for load in loads[6:]:
        load.wait()
    stacked = jnp.concatenate(
        [actions[...].astype(F32), done[...].astype(F32), rewards[...], behaviour[...]], 0
    )
    spread = (
        lax.broadcasted_iota(jnp.int32, (steps, frames), 1) % steps
        == lax.broadcasted_iota(jnp.int32, (steps, frames), 0)
    ).astype(F32)
    env_row = lax.broadcasted_iota(jnp.int32, (envs, frames), 0)
    env_lane = lax.broadcasted_iota(jnp.int32, (envs, frames), 1)
    same_env = env_lane // steps == env_row
    spread = dot(stacked, spread, precision=lax.Precision.HIGHEST).reshape(4, envs, frames)
    flat = jnp.sum(jnp.where(same_env[None], spread, 0.0), 1)

    loads[4].wait()
    loads[5].wait()

    def repack(at, f):
        pair_of = [shards[at, k, :, cols(f)].astype(F32) for k in (0, 1)]
        weights[at, :, cols(f)] = jnp.concatenate(pair_of, 0).astype(BF16)

    def weight_cols(lo, hi):
        return weights[:, :, lo:hi].reshape(units, hi - lo)

    def frame_cols(lo, hi):
        return x[:, :, lo:hi].reshape(frames, hi - lo)

    def layer_one(f, total, own_total):
        lo, hi = edges[f], min(edges[f + 1], feat)
        if lo >= hi:
            return total, own_total
        part = weight_cols(lo, hi)
        one = dot(part, frame_cols(lo, hi), ((1,), (1,)))
        two = dot(own[:, lo:hi], part, ((1,), (1,)))
        return (one, two) if total is None else (total + one, own_total + two)

    total, own_total = None, None
    for s in range(far):
        for f in range(CHUNKS):
            for way in (0, 1):
                if gather_has(way, s, f):
                    gathered(way, s, f).wait_recv()
                    if s + 1 < far and gather_has(way, s + 1, f):
                        gather(way, s + 1, f).start()
                    pair(way, s, f, side).start()
            if s == 0 and f == 0:
                own_pair(other).wait_recv()
            for way in (0, 1):
                if s == 0:
                    if way == 0:
                        repack(chip, f)
                else:
                    pair(way, s - 1, f, other).wait_recv()
                    repack(chip_at(-sign[way] * s), f)
            if s == far - 1 and f > 0:
                way = 0 if f - 1 < half else 1
                pair(way, s, f - 1, other).wait_recv()
                repack(chip_at(-sign[way] * (s + 1)), f - 1)
                total, own_total = layer_one(f - 1, total, own_total)
    way = 0 if CHUNKS - 1 < half else 1
    pair(way, far - 1, CHUNKS - 1, other).wait_recv()
    repack(chip_at(-sign[way] * far), CHUNKS - 1)
    total, own_total = layer_one(CHUNKS - 1, total, own_total)

    second = weight_cols(feat, width)
    second_turned = second.astype(F32).T.astype(BF16)

    def narrow(first):
        act = jnp.maximum(first, 0.0)
        late = dot(act.astype(BF16), second, ((1,), (1,)))
        act = jnp.maximum(late, 0.0) + act
        return dot(act.astype(BF16), head_bf, ((1,), (1,)))

    own_net = narrow(own_total)
    own_out[...] = own_net
    boot = jnp.sum(jnp.where(env_lane == env_row * steps + steps - 1, own_net[:, acts : acts + 1], 0.0), 0, keepdims=True)

    act_one = jnp.maximum(total, 0.0)
    one_bf = act_one.astype(BF16)
    pre_two = dot(second, one_bf)
    two_bf = (jnp.maximum(pre_two, 0.0) + act_one).astype(BF16)
    net = dot(small, two_bf)
    out_grad = trace_gradient(net, boot, flat[0:1], flat[1:2], flat[2:3], flat[3:4], acts, steps).astype(BF16)

    head_grad = dot(out_grad, two_bf, ((1,), (1,)))
    half_units = units // 2
    for k in (0, 1):
        head_part[k] = head_grad[0:24, k * half_units : (k + 1) * half_units]
    hpair = remote(head_part.at[other], head_from, hpair_send, hpair_recv, sibling)
    hpair.start()

    g_two = dot(head_turned[:, :32], out_grad)
    gp_two = jnp.where(pre_two > 0, g_two, 0.0).astype(BF16)
    g_one = g_two + dot(second_turned, gp_two)
    gp_one = jnp.where(total > 0, g_one, 0.0).astype(BF16)

    hpair.wait_recv()
    head_all[chip] = head_part[side] + head_from[...]

    def head_ring(way, s):
        block = head_all.at[chip_at(-sign[way] * s)]
        return remote(block, block, hring_send.at[way, s], hring_recv.at[way, s], ring[way])

    def head_come(way, s):
        block = head_all.at[chip_at(-sign[way] * (s + 1))]
        return remote(block, block, hring_send.at[way, s], hring_recv.at[way, s], ring[way])

    def head_has(way, s):
        return s < far - 1 or way == 0

    for way in (0, 1):
        if head_has(way, 0):
            head_ring(way, 0).start()

    def swap(f):
        return remote(
            for_sibling.at[:, :, cols(f)], from_sibling.at[:, :, cols(f)], half_send.at[f], half_recv.at[f], sibling
        )

    first_side = side == 0
    for f in range(CHUNKS):
        lo, hi = edges[f], edges[f + 1]
        parts = []
        if lo < feat:
            parts.append(dot(gp_one, frame_cols(lo, min(hi, feat))))
        if hi > feat:
            parts.append(dot(gp_two, one_bf, ((1,), (1,))))
        grad = parts[0] if len(parts) == 1 else jnp.concatenate(parts, 1)
        grad = grad.reshape(chips, 2, shard, hi - lo)
        for_sibling[:, :, lo:hi] = jnp.where(first_side, grad[:, 1], grad[:, 0]).astype(BF16)
        swap(f).start()
        mine[:, :, lo:hi] = jnp.where(first_side, grad[:, 0], grad[:, 1])

    def reduce_has(way, s, f):
        return s > 0 or (f < half) == (way == 0)

    def reduce_to(way, s, f):
        return remote(
            sums_out.at[way, s, :, cols(f)], sums_in.at[way, s, :, cols(f)],
            reduce_send.at[way, s, f], reduce_recv.at[way, s, f], ring[way],
        )

    def reduce_step(way, s, f):
        term = mine[chip_at(sign[way] * (far - s)), :, cols(f)]
        if s > 0 and reduce_has(way, s - 1, f):
            reduce_to(way, s - 1, f).wait_recv()
            term = term + sums_in[way, s - 1, :, cols(f)].astype(F32)
        sums_out[way, s, :, cols(f)] = term.astype(BF16)
        reduce_to(way, s, f).start()

    for f in range(CHUNKS):
        swap(f).wait_recv()
        lo, hi = edges[f], edges[f + 1]
        mine[:, :, lo:hi] = mine[:, :, lo:hi] + from_sibling[:, :, lo:hi].astype(F32)
        for way in (0, 1):
            if reduce_has(way, 0, f):
                reduce_step(way, 0, f)

    for s in range(1, far):
        for way in (0, 1):
            if head_has(way, s - 1):
                head_come(way, s - 1).wait_recv()
                if head_has(way, s):
                    head_ring(way, s).start()
        for f in range(CHUNKS):
            for way in (0, 1):
                reduce_step(way, s, f)
        if s == min(2, far - 1):
            for i in range(len(shifts)):
                frames_come(i).wait_recv()
            came = frames_in[...].astype(F32).reshape(agents * SLOTS, feat).astype(BF16)
            answers = narrow(dot(came, weight_cols(0, feat), ((1,), (1,))))
            played_out[...] = answers.reshape(agents, SLOTS, PAD).astype(BF16)
            played_in[agent] = played_out[agent]
            for i in range(len(shifts)):
                remote(
                    played_out.at[to_agent[i]], played_in.at[agent], played_send.at[i], played_recv.at[i], (to_agent[i], dp)
                ).start()

    for way in (0, 1):
        if head_has(way, far - 1):
            head_come(way, far - 1).wait_recv()
    head_final[side] = jnp.sum(head_all[...], 0)
    hlast = remote(head_final.at[side], head_final.at[side], hlast_send, hlast_recv, sibling)
    hlast.start()

    def played_come(i):
        return remote(
            played_out.at[to_agent[i]], played_in.at[from_agent[i]], played_send.at[i], played_recv.at[i], (to_agent[i], dp)
        )

    for i in range(len(shifts)):
        played_come(i).wait_recv()
    back = played_in[...].astype(F32).reshape(agents * SLOTS, PAD).astype(BF16)
    opp_out[...] = dot(placing, back).astype(BF16)

    for f in range(CHUNKS):
        total = mine[chip, :, cols(f)]
        for way in (0, 1):
            reduce_to(way, far - 1, f).wait_recv()
            total = total + sums_in[way, far - 1, :, cols(f)].astype(F32)
        grad_out[:, cols(f)] = total

    remote(head_final.at[other], head_final.at[other], hlast_send, hlast_recv, sibling).wait_recv()
    head_out[...] = head_final[...]

    for s in range(far):
        for f in range(CHUNKS):
            for way in (0, 1):
                if gather_has(way, s, f):
                    gather(way, s, f).wait_send()
                    pair(way, s, f, side).wait_send()
                if reduce_has(way, s, f):
                    reduce_to(way, s, f).wait_send()
        for way in (0, 1):
            if head_has(way, s):
                head_ring(way, s).wait_send()
    own_pair(side).wait_send()
    hpair.wait_send()
    hlast.wait_send()
    for f in range(CHUNKS):
        swap(f).wait_send()
    for i in range(len(shifts)):
        send_frames(i).wait_send()
        played_come(i).wait_send()


def adam_step(master, moment, second, grad, rate):
    moment = beta_first * moment + (1.0 - beta_first) * grad
    second = beta_second * second + (1.0 - beta_second) * grad * grad
    master = master - rate * moment / (jnp.sqrt(second) + adam_eps)
    return (master, moment, second)


def per_device(
    learn_obs, own_obs, opp_obs, opponent, actions, done, rewards, behaviour,
    core_master, core_mom, core_vel, head_master, head_mom, head_vel, rates,
):
    _, envs, steps, feat = learn_obs.shape
    _, shard, width = core_master.shape
    _, head_rows, units = head_master.shape
    agents, dp = lax.axis_size("agent"), lax.axis_size("dp")
    chips = dp // 2
    far = chips // 2
    agent_y = 4 if agents % 4 == 0 else agents
    sizes = (agents, chips, shard, envs, steps, feat, units, head_rows, agent_y)
    vmem, dma = pltpu.VMEM, pltpu.SemaphoreType.DMA
    shifts = agents - 1
    anywhere = pl.BlockSpec(memory_space=pl.ANY)
    in_vmem = pl.BlockSpec(memory_space=vmem)
    grad, head_grad, own_net, opp_net = pl.pallas_call(
        functools.partial(step_kernel, sizes),
        out_shape=(
            jax.ShapeDtypeStruct((shard, width), F32),
            jax.ShapeDtypeStruct((2, 24, units // 2), F32),
            jax.ShapeDtypeStruct((envs, PAD), F32),
            jax.ShapeDtypeStruct((envs, PAD), BF16),
        ),
        in_specs=[anywhere] * 10,
        out_specs=(in_vmem,) * 4,
        scratch_shapes=[
            vmem((envs, steps, feat), BF16),
            vmem((envs, feat), BF16),
            vmem((envs, feat), BF16),
            vmem((envs, 1), jnp.int32),
            vmem((envs, steps), jnp.int32),
            vmem((envs, steps), jnp.int32),
            vmem((envs, steps), F32),
            vmem((envs, steps), F32),
            vmem((shard, width), F32),
            vmem((head_rows, units), F32),
            vmem((chips, 2, shard, width), BF16),
            vmem((chips, 2 * shard, width), BF16),
            vmem((8, 128), F32),
            vmem((chips, shard, width), F32),
            vmem((chips, shard, width), BF16),
            vmem((chips, shard, width), BF16),
            vmem((2, far, shard, width), BF16),
            vmem((2, far, shard, width), BF16),
            vmem((agents, SLOTS, feat), BF16),
            vmem((agents, SLOTS, feat), BF16),
            vmem((agents, SLOTS, PAD), BF16),
            vmem((agents, SLOTS, PAD), BF16),
            vmem((PAD, units), F32),
            vmem((2, 24, units // 2), F32),
            vmem((24, units // 2), F32),
            vmem((chips, 24, units // 2), F32),
            vmem((2, 24, units // 2), F32),
            dma((10,)),
            dma((2, far, CHUNKS)),
            dma((2, far, CHUNKS)),
            dma((2, far, CHUNKS)),
            dma((2, far, CHUNKS)),
            dma,
            dma,
            dma((shifts,)),
            dma((shifts,)),
            dma((shifts,)),
            dma((shifts,)),
            dma((2, far, CHUNKS)),
            dma((2, far, CHUNKS)),
            dma((CHUNKS,)),
            dma((CHUNKS,)),
            dma((2, far)),
            dma((2, far)),
            dma,
            dma,
            dma,
            dma,
        ],
        compiler_params=pltpu.CompilerParams(
            collective_id=0, has_side_effects=True, vmem_limit_bytes=56 * 2**20
        ),
    )(learn_obs, own_obs, opp_obs, opponent, actions, done, rewards, behaviour, core_master, head_master)
    head_total = jnp.concatenate([head_grad[0, :head_rows], head_grad[1, :head_rows]], 1)
    rate = rates[0]
    new_core = adam_step(core_master[0], core_mom[0], core_vel[0], grad, rate)
    new_head = adam_step(head_master[0], head_mom[0], head_vel[0], head_total, rate)
    return (
        own_net[None, :, : head_rows - 1],
        opp_net[None, :, : head_rows - 1],
        *[a[None] for a in new_core],
        *[a[None] for a in new_head],
    )


def solution(mesh):
    rows, whole = P("agent", "dp"), P("agent")
    return jax.shard_map(
        per_device,
        mesh=mesh,
        in_specs=(rows,) * 11 + (whole,) * 4,
        out_specs=(rows,) * 5 + (whole,) * 3,
        check_vma=False,
    )
```

```python
import functools

import jax
import jax.numpy as jnp
from jax import lax
from jax.experimental import pallas as pl
from jax.experimental.pallas import tpu as pltpu
from jax.sharding import PartitionSpec as P

MESH = pl.DeviceIdType.MESH
F32 = jnp.float32
BF16 = jnp.bfloat16
SLOTS = 8
PAD = 128
CHUNKS = 4

gamma_rate = 0.99
baseline_cost = 0.5
entropy_cost = 0.05
beta_first = 0.9
beta_second = 0.99
adam_eps = 1e-08


def dot(left, right, dims=((1,), (0,)), precision=None):
    return lax.dot_general(left, right, (dims, ((), ())), precision=precision, preferred_element_type=F32)


def bounds(total, parts, unit=128):
    units = -(-total // unit)
    return [min(total, unit * (units * i // parts)) for i in range(parts + 1)]


def turned(x):
    return x.swapaxes(1, 2)


def column(row_vector, sublanes):
    return jnp.broadcast_to(row_vector, (sublanes, row_vector.shape[1]))


def trace_gradient(out, boot, actions, done, rewards, behaviour, actions_total, steps):
    rows, frames = out.shape
    scale = 1.0 / steps
    row = lax.broadcasted_iota(jnp.int32, (rows, frames), 0)
    time = lax.broadcasted_iota(jnp.int32, (8, frames), 1) % steps
    is_logit = row < actions_total
    values = column(out[actions_total : actions_total + 1, :], 8)
    total = jnp.sum(jnp.where(is_logit, jnp.exp(out), 0.0), 0, keepdims=True)
    logp = out - jnp.log(total)
    probs = jnp.where(is_logit, jnp.exp(logp), 0.0)
    chosen = (row.astype(F32) == actions).astype(F32)
    logp_act = jnp.sum(jnp.where(is_logit, logp, 0.0) * chosen, 0, keepdims=True)
    entropy = -jnp.sum(probs * jnp.where(is_logit, logp, 0.0), 0, keepdims=True)
    ratio = column(jnp.minimum(1.0, jnp.exp(logp_act - behaviour)), 8)
    discount = column(gamma_rate * (1.0 - done), 8)
    rewards, boot = column(rewards, 8), column(boot, 8)
    last = time == steps - 1

    def later(x, by):
        return pltpu.roll(x, frames - by, 1)

    next_values = jnp.where(last, boot, later(values, 1))
    corr = ratio * (rewards + discount * next_values - values)
    factor = discount * ratio
    by = 1
    while by < steps:
        inside = time < steps - by
        corr, factor = (
            corr + factor * jnp.where(inside, later(corr, by), 0.0),
            factor * jnp.where(inside, later(factor, by), 0.0),
        )
        by *= 2
    targets = values + corr
    next_targets = jnp.where(last, boot, later(targets, 1))
    advantage = ratio * (rewards + discount * next_targets - values)
    grad_logits = scale * (
        -advantage[:1] * (chosen - probs) + entropy_cost * probs * (logp + entropy)
    )
    grad_value = scale * (-baseline_cost * (targets - values))[:1]
    return jnp.where(is_logit, grad_logits, jnp.where(row == actions_total, grad_value, 0.0))


def step_kernel(
    sizes,
    learn_hbm, own_hbm, opp_hbm, opponent_hbm, actions_hbm, done_hbm, rewards_hbm, behaviour_hbm, core_hbm, head_hbm,
    grad_out, head_out, own_out, opp_out,
    x, own, opp, opponent, actions, done, rewards, behaviour, core, head,
    shards, weights, mine, for_sibling, from_sibling, sums_out, sums_in, frames_out, frames_in,
    played_out, played_in, heads, head_part, head_from, head_all, head_final,
    load_sem, gather_send, gather_recv, pair_send, pair_recv, own_send, own_recv,
    frame_send, frame_recv, played_send, played_recv, reduce_send, reduce_recv,
    half_send, half_recv, hring_send, hring_recv, hpair_send, hpair_recv, hlast_send, hlast_recv,
):
    (agents, chips, shard, envs, steps, feat, units, head_rows, agent_y) = sizes
    frames = envs * steps
    width = feat + units
    acts = head_rows - 1
    edges = bounds(width, CHUNKS)
    far = chips // 2
    half = CHUNKS // 2
    stages = far // 2
    agent, dp = lax.axis_index("agent"), lax.axis_index("dp")
    chip, side = dp // 2, dp % 2
    other = 1 - side
    agent_x = agents // agent_y
    ax, ay = agent // agent_y, agent % agent_y

    def chip_at(offset):
        return lax.rem(chip + (offset + 2 * chips), chips)

    sibling = (agent, 2 * chip + other)
    sign = [1, -1]
    next_one = [(agent, 2 * chip_at(k) + side) for k in sign]
    next_two = [(agent, 2 * chip_at(2 * k) + side) for k in sign]
    target = [next_two, next_one]
    shifts = [(i, j) for i in range(agent_x) for j in range(agent_y) if (i, j) != (0, 0)]
    to_agent = [lax.rem(ax + i, agent_x) * agent_y + lax.rem(ay + j, agent_y) for i, j in shifts]
    from_agent = [lax.rem(ax + agent_x - i, agent_x) * agent_y + lax.rem(ay + agent_y - j, agent_y) for i, j in shifts]

    barrier = pltpu.get_barrier_semaphore()
    peers = [sibling, *next_one, *next_two, *[(a, dp) for a in to_agent]]
    for peer in peers:
        pl.semaphore_signal(barrier, inc=1, device_id=peer, device_id_type=MESH)

    loads = [
        pltpu.make_async_copy(src, dst, load_sem.at[i])
        for i, (src, dst) in enumerate((
            (core_hbm.at[0], core), (head_hbm, head), (opponent_hbm.at[0], opponent), (opp_hbm.at[0], opp),
            (learn_hbm.at[0], x), (own_hbm.at[0], own), (actions_hbm.at[0], actions), (done_hbm.at[0], done),
            (rewards_hbm.at[0], rewards), (behaviour_hbm.at[0], behaviour),
        ))
    ]
    for load in loads:
        load.start()

    def cols(f):
        return pl.ds(edges[f], edges[f + 1] - edges[f])

    def remote(src, dst, send, recv, to):
        return pltpu.make_async_remote_copy(
            src_ref=src, dst_ref=dst, send_sem=send, recv_sem=recv, device_id=to, device_id_type=MESH
        )

    kinds = (0, 1)

    def gather_has(way, kind, i, f):
        return kind == 1 or i < stages - 1 or (f < half) == (way == 0)

    def gather(way, kind, i, f):
        block = shards.at[chip_at(-sign[way] * 2 * i), side, :, cols(f)]
        at = (way, kind, i, f)
        return remote(block, block, gather_send.at[at], gather_recv.at[at], target[kind][way])

    def came_from(way, kind, i):
        return chip_at(-sign[way] * (2 * i + 2 - kind))

    def gathered(way, kind, i, f):
        block = shards.at[came_from(way, kind, i), side, :, cols(f)]
        at = (way, kind, i, f)
        return remote(block, block, gather_send.at[at], gather_recv.at[at], target[kind][way])

    def pair(way, kind, i, f, which):
        block = shards.at[came_from(way, kind, i), which, :, cols(f)]
        at = (way, kind, i, f)
        return remote(block, block, pair_send.at[at], pair_recv.at[at], sibling)

    def own_pair(which):
        block = shards.at[chip, which]
        return remote(block, block, own_send, own_recv, sibling)

    loads[2].wait()
    ids = opponent[...]
    agent_row = lax.broadcasted_iota(jnp.int32, (PAD, envs), 0)
    member = (ids == agent_row).astype(F32)
    before = (
        lax.broadcasted_iota(jnp.int32, (envs, envs), 0) < lax.broadcasted_iota(jnp.int32, (envs, envs), 1)
    ).astype(BF16)
    ranks = jnp.sum(dot(member.astype(BF16), before) * member, 0, keepdims=True)
    position = ids * SLOTS + ranks.astype(jnp.int32)
    slot_row = lax.broadcasted_iota(jnp.int32, (agents * SLOTS, envs), 0)
    placed = (position == slot_row).astype(BF16)
    loads[0].wait()
    shards[chip, side] = core[...].astype(BF16)
    loads[3].wait()
    frames_out[...] = dot(placed, opp[...]).reshape(agents, SLOTS, feat).astype(BF16)

    pl.semaphore_wait(barrier, len(peers))
    for kind in kinds:
        for f in range(CHUNKS):
            for way in (0, 1):
                if gather_has(way, kind, 0, f):
                    gather(way, kind, 0, f).start()
    own_pair(side).start()

    def send_frames(i):
        return remote(
            frames_out.at[to_agent[i]], frames_in.at[agent], frame_send.at[i], frame_recv.at[i], (to_agent[i], dp)
        )

    def frames_come(i):
        return remote(
            frames_out.at[to_agent[i]], frames_in.at[from_agent[i]], frame_send.at[i], frame_recv.at[i], (to_agent[i], dp)
        )

    for i in range(len(shifts)):
        send_frames(i).start()
    frames_in[agent] = frames_out[agent]

    loads[1].wait()
    heads[...] = jnp.zeros_like(heads)
    for i in range(head_rows):
        heads[i : i + 1, :] = head[i]
    head_bf = heads[...].astype(BF16)
    head_turned = heads[...].T.astype(BF16)
    small = head_bf[:32]

    for load in loads[6:]:
        load.wait()
    stacked = jnp.concatenate(
        [actions[...].astype(F32), done[...].astype(F32), rewards[...], behaviour[...]], 0
    )
    env_lane = lax.broadcasted_iota(jnp.int32, (envs, frames), 1)
    to_frames = (env_lane // steps == lax.broadcasted_iota(jnp.int32, (envs, frames), 0)).astype(F32)
    spread = dot(stacked, to_frames, precision=lax.Precision.HIGHEST).reshape(4, steps, frames)
    same_step = (
        lax.broadcasted_iota(jnp.int32, (steps, frames), 1) % steps
        == lax.broadcasted_iota(jnp.int32, (steps, frames), 0)
    )
    flat = jnp.sum(jnp.where(same_step[None], spread, 0.0), 1)

    loads[4].wait()
    loads[5].wait()

    def repack(at, f):
        pair_of = [shards[at, k, :, cols(f)].astype(F32) for k in (0, 1)]
        weights[at, :, cols(f)] = jnp.concatenate(pair_of, 0).astype(BF16)

    def weight_cols(lo, hi):
        return weights[:, :, lo:hi].reshape(units, hi - lo)

    def frame_cols(lo, hi):
        return x[:, :, lo:hi].reshape(frames, hi - lo)

    def layer_one(f, total, own_total):
        lo, hi = edges[f], min(edges[f + 1], feat)
        if lo >= hi:
            return total, own_total
        part = weight_cols(lo, hi)
        one = dot(part, frame_cols(lo, hi), ((1,), (1,)))
        two = dot(own[:, lo:hi], part, ((1,), (1,)))
        return (one, two) if total is None else (total + one, own_total + two)

    total, own_total = None, None

    def forwarded(i, f):
        for kind in kinds:
            for way in (0, 1):
                if gather_has(way, kind, i, f):
                    pair(way, kind, i, f, other).wait_recv()
                    repack(came_from(way, kind, i), f)

    for i in range(stages):
        for f in range(CHUNKS):
            for kind in kinds:
                for way in (0, 1):
                    if gather_has(way, kind, i, f):
                        gathered(way, kind, i, f).wait_recv()
                        if kind == 0 and i + 1 < stages:
                            for later in kinds:
                                if gather_has(way, later, i + 1, f):
                                    gather(way, later, i + 1, f).start()
                        pair(way, kind, i, f, side).start()
            if i == 0:
                if f == 0:
                    own_pair(other).wait_recv()
                repack(chip, f)
            else:
                forwarded(i - 1, f)
            if i == stages - 1 and f > 0:
                forwarded(i, f - 1)
                total, own_total = layer_one(f - 1, total, own_total)
    forwarded(stages - 1, CHUNKS - 1)
    total, own_total = layer_one(CHUNKS - 1, total, own_total)

    second = weight_cols(feat, width)
    second_turned = second.astype(F32).T.astype(BF16)

    def narrow(first):
        act = jnp.maximum(first, 0.0)
        late = dot(act.astype(BF16), second, ((1,), (1,)))
        act = jnp.maximum(late, 0.0) + act
        return dot(head_bf, act.astype(BF16), ((1,), (1,)))

    own_net = narrow(own_total)
    own_out[...] = own_net[:32]
    boot = dot(column(own_net[acts : acts + 1], 8), to_frames, precision=lax.Precision.HIGHEST)[:1]

    act_one = jnp.maximum(total, 0.0)
    one_bf = act_one.astype(BF16)
    pre_two = dot(second, one_bf)
    two_bf = (jnp.maximum(pre_two, 0.0) + act_one).astype(BF16)
    net = dot(small, two_bf)
    out_grad = trace_gradient(net, boot, flat[0:1], flat[1:2], flat[2:3], flat[3:4], acts, steps).astype(BF16)

    head_grad = dot(out_grad, two_bf, ((1,), (1,)))
    half_units = units // 2
    for k in (0, 1):
        head_part[k] = head_grad[:, k * half_units : (k + 1) * half_units].astype(BF16)
    hpair = remote(head_part.at[other], head_from, hpair_send, hpair_recv, sibling)
    hpair.start()

    g_two = dot(head_turned[:, :32], out_grad)
    gp_two = jnp.where(pre_two > 0, g_two, 0.0).astype(BF16)
    g_one = g_two + dot(second_turned, gp_two)
    gp_one = jnp.where(total > 0, g_one, 0.0).astype(BF16)

    hpair.wait_recv()
    head_all[chip] = (head_part[side].astype(F32) + head_from[...].astype(F32)).astype(BF16)

    def head_has(way, kind, i):
        return kind == 1 or i < stages - 1 or way == 0

    def head_ring(way, kind, i):
        block = head_all.at[chip_at(-sign[way] * 2 * i)]
        at = (way, kind, i)
        return remote(block, block, hring_send.at[at], hring_recv.at[at], target[kind][way])

    def head_come(way, kind, i):
        block = head_all.at[came_from(way, kind, i)]
        at = (way, kind, i)
        return remote(block, block, hring_send.at[at], hring_recv.at[at], target[kind][way])

    def head_step(i):
        for kind in kinds:
            for way in (0, 1):
                if head_has(way, kind, i):
                    head_come(way, kind, i).wait_recv()
                    if kind == 0 and i + 1 < stages:
                        for later in kinds:
                            if head_has(way, later, i + 1):
                                head_ring(way, later, i + 1).start()

    for kind in kinds:
        for way in (0, 1):
            if head_has(way, kind, 0):
                head_ring(way, kind, 0).start()

    def swap(f):
        return remote(
            for_sibling.at[:, :, cols(f)], from_sibling.at[:, :, cols(f)], half_send.at[f], half_recv.at[f], sibling
        )

    first_side = side == 0
    for f in range(CHUNKS):
        lo, hi = edges[f], edges[f + 1]
        parts = []
        if lo < feat:
            parts.append(dot(gp_one, frame_cols(lo, min(hi, feat))))
        if hi > feat:
            parts.append(dot(gp_two, one_bf, ((1,), (1,))))
        grad = parts[0] if len(parts) == 1 else jnp.concatenate(parts, 1)
        grad = grad.reshape(chips, 2, shard, hi - lo)
        for_sibling[:, :, lo:hi] = jnp.where(first_side, grad[:, 1], grad[:, 0]).astype(BF16)
        swap(f).start()
        mine[:, :, lo:hi] = jnp.where(first_side, grad[:, 0], grad[:, 1])

    def reduce_has(way, kind, i, f):
        return kind == 1 or i > 0 or (f < half) == (way == 0)

    def reduce_to(way, kind, i, f):
        at = (way, kind, i)
        return remote(
            sums_out.at[(*at, slice(None), cols(f))], sums_in.at[(*at, slice(None), cols(f))],
            reduce_send.at[(*at, f)], reduce_recv.at[(*at, f)], target[kind][way],
        )

    def arrived(way, i, f, term):
        for kind in kinds:
            if reduce_has(way, kind, i, f):
                reduce_to(way, kind, i, f).wait_recv()
                term = term + sums_in[way, kind, i, :, cols(f)].astype(F32)
        return term

    def reduce_step(way, i, f):
        for kind in kinds:
            if reduce_has(way, kind, i, f):
                term = mine[chip_at(sign[way] * (far - 2 * i - kind)), :, cols(f)]
                if kind == 0 and i > 0:
                    term = arrived(way, i - 1, f, term)
                sums_out[way, kind, i, :, cols(f)] = term.astype(BF16)
                reduce_to(way, kind, i, f).start()

    for f in range(CHUNKS):
        swap(f).wait_recv()
        lo, hi = edges[f], edges[f + 1]
        mine[:, :, lo:hi] = mine[:, :, lo:hi] + from_sibling[:, :, lo:hi].astype(F32)
        for way in (0, 1):
            reduce_step(way, 0, f)

    def play():
        for i in range(len(shifts)):
            frames_come(i).wait_recv()
        came = frames_in[...].astype(F32).reshape(agents * SLOTS, feat).astype(BF16)
        act = jnp.maximum(dot(came, weight_cols(0, feat), ((1,), (1,))), 0.0)
        late = dot(act.astype(BF16), second, ((1,), (1,)))
        act = jnp.maximum(late, 0.0) + act
        answers = dot(act.astype(BF16), head_bf, ((1,), (1,)))
        played_out[...] = answers.reshape(agents, SLOTS, PAD).astype(BF16)
        for i in range(len(shifts)):
            remote(
                played_out.at[to_agent[i]], played_in.at[agent], played_send.at[i], played_recv.at[i], (to_agent[i], dp)
            ).start()
        played_in[agent] = played_out[agent]

    play()
    for i in range(1, stages):
        head_step(i - 1)
        for f in range(CHUNKS):
            for way in (0, 1):
                reduce_step(way, i, f)

    head_step(stages - 1)
    head_final[side] = jnp.sum(head_all[...].astype(F32), 0)
    hlast = remote(head_final.at[side], head_final.at[side], hlast_send, hlast_recv, sibling)
    hlast.start()

    def played_come(i):
        return remote(
            played_out.at[to_agent[i]], played_in.at[from_agent[i]], played_send.at[i], played_recv.at[i], (to_agent[i], dp)
        )

    for i in range(len(shifts)):
        played_come(i).wait_recv()
    back = played_in[...].astype(F32).reshape(agents * SLOTS, PAD).T.astype(BF16)
    opp_out[...] = dot(back, placed)[:32].astype(BF16)

    for f in range(CHUNKS):
        total = mine[chip, :, cols(f)]
        for way in (0, 1):
            total = arrived(way, stages - 1, f, total)
        grad_out[:, cols(f)] = total

    remote(head_final.at[other], head_final.at[other], hlast_send, hlast_recv, sibling).wait_recv()
    head_out[...] = head_final[...]

    for i in range(stages):
        for kind in kinds:
            for way in (0, 1):
                for f in range(CHUNKS):
                    if gather_has(way, kind, i, f):
                        gather(way, kind, i, f).wait_send()
                        pair(way, kind, i, f, side).wait_send()
                    if reduce_has(way, kind, i, f):
                        reduce_to(way, kind, i, f).wait_send()
                if head_has(way, kind, i):
                    head_ring(way, kind, i).wait_send()
    own_pair(side).wait_send()
    hpair.wait_send()
    hlast.wait_send()
    for f in range(CHUNKS):
        swap(f).wait_send()
    for i in range(len(shifts)):
        send_frames(i).wait_send()
        played_come(i).wait_send()


def adam_step(master, moment, second, grad, rate):
    moment = beta_first * moment + (1.0 - beta_first) * grad
    second = beta_second * second + (1.0 - beta_second) * grad * grad
    master = master - rate * moment / (jnp.sqrt(second) + adam_eps)
    return (master, moment, second)


def finish_kernel(
    head_rows, rate, grad, head_grad, own_net, opp_net, core, core_mom, core_vel, head, head_mom, head_vel,
    own_out, opp_out, new_core, new_mom, new_vel, new_head, new_head_mom, new_head_vel,
):
    by = rate[0]
    new_core[0], new_mom[0], new_vel[0] = adam_step(core[0], core_mom[0], core_vel[0], grad[...], by)
    for i in range(head_rows):
        row = jnp.concatenate([head_grad[0, i : i + 1], head_grad[1, i : i + 1]], 1)
        new_head[i], new_head_mom[i], new_head_vel[i] = adam_step(head[i], head_mom[i], head_vel[i], row, by)
    for i in range(head_rows - 1):
        own_out[i] = own_net[i : i + 1]
    opp_out[0] = opp_net[0 : head_rows - 1]


def per_device(
    learn_obs, own_obs, opp_obs, opponent, actions, done, rewards, behaviour,
    core_master, core_mom, core_vel, head_master, head_mom, head_vel, rates,
):
    _, envs, steps, feat = learn_obs.shape
    _, shard, width = core_master.shape
    _, head_rows, units = head_master.shape
    agents, dp = lax.axis_size("agent"), lax.axis_size("dp")
    chips = dp // 2
    far = chips // 2
    stages = far // 2
    agent_y = 4 if agents % 4 == 0 else agents
    sizes = (agents, chips, shard, envs, steps, feat, units, head_rows, agent_y)
    vmem, dma = pltpu.VMEM, pltpu.SemaphoreType.DMA
    shifts = max(1, agents - 1)
    anywhere = pl.BlockSpec(memory_space=pl.ANY)
    in_vmem = pl.BlockSpec(memory_space=vmem)
    head_rows_first = [a.swapaxes(0, 1) for a in (head_master, head_mom, head_vel)]
    grad, head_grad, own_net, opp_net = pl.pallas_call(
        functools.partial(step_kernel, sizes),
        out_shape=(
            jax.ShapeDtypeStruct((shard, width), F32),
            jax.ShapeDtypeStruct((2, 32, units // 2), F32),
            jax.ShapeDtypeStruct((32, envs), F32),
            jax.ShapeDtypeStruct((32, envs), BF16),
        ),
        in_specs=[anywhere] * 10,
        out_specs=(in_vmem,) * 4,
        scratch_shapes=[
            vmem((envs, steps, feat), BF16),
            vmem((envs, feat), BF16),
            vmem((envs, feat), BF16),
            vmem((1, envs), jnp.int32),
            vmem((steps, envs), jnp.int32),
            vmem((steps, envs), jnp.int32),
            vmem((steps, envs), F32),
            vmem((steps, envs), F32),
            vmem((shard, width), F32),
            vmem((head_rows, 1, units), F32),
            vmem((chips, 2, shard, width), BF16),
            vmem((chips, 2 * shard, width), BF16),
            vmem((chips, shard, width), F32),
            vmem((chips, shard, width), BF16),
            vmem((chips, shard, width), BF16),
            vmem((2, 2, stages, shard, width), BF16),
            vmem((2, 2, stages, shard, width), BF16),
            vmem((agents, SLOTS, feat), BF16),
            vmem((agents, SLOTS, feat), BF16),
            vmem((agents, SLOTS, PAD), BF16),
            vmem((agents, SLOTS, PAD), BF16),
            vmem((PAD, units), F32),
            vmem((2, 32, units // 2), BF16),
            vmem((32, units // 2), BF16),
            vmem((chips, 32, units // 2), BF16),
            vmem((2, 32, units // 2), F32),
            dma((10,)),
            dma((2, 2, stages, CHUNKS)),
            dma((2, 2, stages, CHUNKS)),
            dma((2, 2, stages, CHUNKS)),
            dma((2, 2, stages, CHUNKS)),
            dma,
            dma,
            dma((shifts,)),
            dma((shifts,)),
            dma((shifts,)),
            dma((shifts,)),
            dma((2, 2, stages, CHUNKS)),
            dma((2, 2, stages, CHUNKS)),
            dma((CHUNKS,)),
            dma((CHUNKS,)),
            dma((2, 2, stages)),
            dma((2, 2, stages)),
            dma,
            dma,
            dma,
            dma,
        ],
        compiler_params=pltpu.CompilerParams(
            collective_id=0, has_side_effects=True, vmem_limit_bytes=56 * 2**20
        ),
    )(
        learn_obs, own_obs, opp_obs, turned(opponent), turned(actions), turned(done), turned(rewards), turned(behaviour),
        core_master, head_rows_first[0],
    )
    own_logits, opp_logits, *new = pl.pallas_call(
        functools.partial(finish_kernel, head_rows),
        out_shape=(
            jax.ShapeDtypeStruct((head_rows - 1, 1, envs), F32),
            jax.ShapeDtypeStruct((1, head_rows - 1, envs), BF16),
            *[jax.ShapeDtypeStruct((1, shard, width), F32)] * 3,
            *[jax.ShapeDtypeStruct((head_rows, 1, units), F32)] * 3,
        ),
        in_specs=[pl.BlockSpec(memory_space=pltpu.SMEM)] + [in_vmem] * 10,
        out_specs=(in_vmem,) * 8,
        compiler_params=pltpu.CompilerParams(vmem_limit_bytes=8 * 2**20),
    )(rates, grad, head_grad, own_net, opp_net, core_master, core_mom, core_vel, *head_rows_first)
    return (
        own_logits.transpose(1, 2, 0),
        turned(opp_logits),
        *new[:3],
        *[a.swapaxes(0, 1) for a in new[3:]],
    )


def solution(mesh):
    rows, whole = P("agent", "dp"), P("agent")
    return jax.shard_map(
        per_device,
        mesh=mesh,
        in_specs=(rows,) * 11 + (whole,) * 4,
        out_specs=(rows,) * 5 + (whole,) * 3,
        check_vma=False,
    )
```

```python
import functools

import jax
import jax.numpy as jnp
from jax import lax
from jax.experimental import pallas as pl
from jax.experimental.pallas import tpu as pltpu
from jax.sharding import PartitionSpec as P

MESH = pl.DeviceIdType.MESH
F32 = jnp.float32
BF16 = jnp.bfloat16
SLOTS = 8
PAD = 128
CHUNKS = 3

gamma_rate = 0.99
baseline_cost = 0.5
entropy_cost = 0.05
beta_first = 0.9
beta_second = 0.99
adam_eps = 1e-08


def dot(left, right, dims=((1,), (0,)), precision=None):
    return lax.dot_general(left, right, (dims, ((), ())), precision=precision, preferred_element_type=F32)


def bounds(total, parts, unit=128):
    units = -(-total // unit)
    return [min(total, unit * (units * i // parts)) for i in range(parts + 1)]


def turned(x):
    return x.swapaxes(1, 2)


def column(row_vector, sublanes):
    return jnp.broadcast_to(row_vector, (sublanes, row_vector.shape[1]))


def trace_gradient(out, boot, actions, done, rewards, behaviour, actions_total, steps):
    rows, frames = out.shape
    scale = 1.0 / steps
    row = lax.broadcasted_iota(jnp.int32, (rows, frames), 0)
    time = lax.broadcasted_iota(jnp.int32, (8, frames), 1) % steps
    is_logit = row < actions_total
    values = column(out[actions_total : actions_total + 1, :], 8)
    total = jnp.sum(jnp.where(is_logit, jnp.exp(out), 0.0), 0, keepdims=True)
    logp = out - jnp.log(total)
    probs = jnp.where(is_logit, jnp.exp(logp), 0.0)
    chosen = (row.astype(F32) == actions).astype(F32)
    logp_act = jnp.sum(jnp.where(is_logit, logp, 0.0) * chosen, 0, keepdims=True)
    entropy = -jnp.sum(probs * jnp.where(is_logit, logp, 0.0), 0, keepdims=True)
    ratio = column(jnp.minimum(1.0, jnp.exp(logp_act - behaviour)), 8)
    discount = column(gamma_rate * (1.0 - done), 8)
    rewards, boot = column(rewards, 8), column(boot, 8)
    last = time == steps - 1

    def later(x, by):
        return pltpu.roll(x, frames - by, 1)

    next_values = jnp.where(last, boot, later(values, 1))
    corr = ratio * (rewards + discount * next_values - values)
    factor = discount * ratio
    by = 1
    while by < steps:
        inside = time < steps - by
        corr, factor = (
            corr + factor * jnp.where(inside, later(corr, by), 0.0),
            factor * jnp.where(inside, later(factor, by), 0.0),
        )
        by *= 2
    targets = values + corr
    next_targets = jnp.where(last, boot, later(targets, 1))
    advantage = ratio * (rewards + discount * next_targets - values)
    grad_logits = scale * (
        -advantage[:1] * (chosen - probs) + entropy_cost * probs * (logp + entropy)
    )
    grad_value = scale * (-baseline_cost * (targets - values))[:1]
    return jnp.where(is_logit, grad_logits, jnp.where(row == actions_total, grad_value, 0.0))


def step_kernel(
    sizes,
    learn_hbm, own_hbm, opp_hbm, opponent_hbm, actions_hbm, done_hbm, rewards_hbm, behaviour_hbm, core_hbm, head_hbm,
    grad_out, head_out, own_out, opp_out,
    x, own, opp, opponent, actions, done, rewards, behaviour, core, head,
    shards, weights, mine, for_sibling, from_sibling, sums_out, sums_in, frames_out, frames_mid, frames_in,
    played_out, played_mid, played_in, heads, head_part, head_from, head_all, head_final,
    load_sem, gather_send, gather_recv, pair_send, pair_recv, own_send, own_recv,
    frame_send, frame_recv, played_send, played_recv, reduce_send, reduce_recv,
    half_send, half_recv, hring_send, hring_recv, hpair_send, hpair_recv, hlast_send, hlast_recv,
):
    (agents, chips, shard, envs, steps, feat, units, head_rows, agent_y) = sizes
    frames = envs * steps
    width = feat + units
    acts = head_rows - 1
    edges = bounds(width, CHUNKS)
    far = chips // 2
    half = CHUNKS // 2
    stages = far // 2
    agent, dp = lax.axis_index("agent"), lax.axis_index("dp")
    chip, side = dp // 2, dp % 2
    other = 1 - side
    agent_x = agents // agent_y
    ax, ay = agent // agent_y, agent % agent_y

    def chip_at(offset):
        return lax.rem(chip + (offset + 2 * chips), chips)

    sibling = (agent, 2 * chip + other)
    sign = [1, -1]
    next_one = [(agent, 2 * chip_at(k) + side) for k in sign]
    next_two = [(agent, 2 * chip_at(2 * k) + side) for k in sign]
    target = [next_two, next_one]
    x_to = [lax.rem(ax + i, agent_x) for i in range(1, agent_x)]
    x_from = [lax.rem(ax + agent_x - i, agent_x) for i in range(1, agent_x)]
    y_to = [lax.rem(ay + i, agent_y) for i in range(1, agent_y)]
    y_from = [lax.rem(ay + agent_y - i, agent_y) for i in range(1, agent_y)]
    x_peer = [(k * agent_y + ay, dp) for k in x_to]
    y_peer = [(ax * agent_y + k, dp) for k in y_to]

    barrier = pltpu.get_barrier_semaphore()
    peers = [*next_two, *next_one, *x_peer, *y_peer, sibling]
    for peer in peers:
        pl.semaphore_signal(barrier, inc=1, device_id=peer, device_id_type=MESH)

    loads = [
        pltpu.make_async_copy(src, dst, load_sem.at[i])
        for i, (src, dst) in enumerate((
            (core_hbm.at[0], core), (head_hbm, head), (opponent_hbm.at[0], opponent), (opp_hbm.at[0], opp),
            (learn_hbm.at[0], x), (own_hbm.at[0], own), (actions_hbm.at[0], actions), (done_hbm.at[0], done),
            (rewards_hbm.at[0], rewards), (behaviour_hbm.at[0], behaviour),
        ))
    ]
    for load in loads:
        load.start()

    def cols(f):
        return pl.ds(edges[f], edges[f + 1] - edges[f])

    def remote(src, dst, send, recv, to):
        return pltpu.make_async_remote_copy(
            src_ref=src, dst_ref=dst, send_sem=send, recv_sem=recv, device_id=to, device_id_type=MESH
        )

    kinds = (0, 1)

    def gather_has(way, kind, i, f):
        return kind == 1 or i < stages - 1 or (f < half) == (way == 0)

    def gather(way, kind, i, f):
        block = shards.at[chip_at(-sign[way] * 2 * i), side, :, cols(f)]
        at = (way, kind, i, f)
        return remote(block, block, gather_send.at[at], gather_recv.at[at], target[kind][way])

    def came_from(way, kind, i):
        return chip_at(-sign[way] * (2 * i + 2 - kind))

    def gathered(way, kind, i, f):
        block = shards.at[came_from(way, kind, i), side, :, cols(f)]
        at = (way, kind, i, f)
        return remote(block, block, gather_send.at[at], gather_recv.at[at], target[kind][way])

    def pair(way, kind, i, f, which):
        block = shards.at[came_from(way, kind, i), which, :, cols(f)]
        at = (way, kind, i, f)
        return remote(block, block, pair_send.at[at], pair_recv.at[at], sibling)

    def own_pair(which):
        block = shards.at[chip, which]
        return remote(block, block, own_send, own_recv, sibling)

    loads[0].wait()
    shards[chip, side] = core[...].astype(BF16)

    pl.semaphore_wait(barrier, len(peers))
    for kind in kinds:
        for f in range(CHUNKS):
            for way in (0, 1):
                if gather_has(way, kind, 0, f):
                    gather(way, kind, 0, f).start()
    own_pair(side).start()

    loads[2].wait()
    ids = opponent[...]
    agent_row = lax.broadcasted_iota(jnp.int32, (PAD, envs), 0)
    member = (ids == agent_row).astype(F32)
    before = (
        lax.broadcasted_iota(jnp.int32, (envs, envs), 0) < lax.broadcasted_iota(jnp.int32, (envs, envs), 1)
    ).astype(BF16)
    ranks = jnp.sum(dot(member.astype(BF16), before) * member, 0, keepdims=True)
    position = ids * SLOTS + ranks.astype(jnp.int32)
    slot_row = lax.broadcasted_iota(jnp.int32, (agents * SLOTS, envs), 0)
    placed = (position == slot_row).astype(BF16)
    loads[3].wait()
    frames_out[...] = dot(placed, opp[...]).reshape(agent_x, agent_y, SLOTS, feat).astype(BF16)

    def frames_x(i, at):
        return remote(frames_out.at[x_to[i]], frames_mid.at[at], frame_send.at[0, i], frame_recv.at[0, i], x_peer[i])

    def frames_y(i, at):
        return remote(
            frames_mid.at[:, y_to[i]], frames_in.at[:, at], frame_send.at[1, i], frame_recv.at[1, i], y_peer[i]
        )

    for i in range(agent_x - 1):
        frames_x(i, ax).start()
    frames_mid[ax] = frames_out[ax]

    def frames_on():
        for i in range(agent_x - 1):
            frames_x(i, x_from[i]).wait_recv()
        for i in range(agent_y - 1):
            frames_y(i, ay).start()
        frames_in[:, ay] = frames_mid[:, ay]


    loads[1].wait()
    heads[...] = jnp.zeros_like(heads)
    for i in range(head_rows):
        heads[i : i + 1, :] = head[i]
    head_bf = heads[...].astype(BF16)
    head_turned = heads[...].T.astype(BF16)
    small = head_bf[:32]

    for load in loads[6:]:
        load.wait()
    stacked = jnp.concatenate(
        [actions[...].astype(F32), done[...].astype(F32), rewards[...], behaviour[...]], 0
    )
    env_lane = lax.broadcasted_iota(jnp.int32, (envs, frames), 1)
    to_frames = (env_lane // steps == lax.broadcasted_iota(jnp.int32, (envs, frames), 0)).astype(F32)
    spread = dot(stacked, to_frames, precision=lax.Precision.HIGHEST).reshape(4, steps, frames)
    same_step = (
        lax.broadcasted_iota(jnp.int32, (steps, frames), 1) % steps
        == lax.broadcasted_iota(jnp.int32, (steps, frames), 0)
    )
    flat = jnp.sum(jnp.where(same_step[None], spread, 0.0), 1)

    loads[4].wait()
    loads[5].wait()

    def repack(at, f):
        pair_of = [shards[at, k, :, cols(f)].astype(F32) for k in (0, 1)]
        weights[at, :, cols(f)] = jnp.concatenate(pair_of, 0).astype(BF16)

    def weight_cols(lo, hi):
        return weights[:, :, lo:hi].reshape(units, hi - lo)

    def frame_cols(lo, hi):
        return x[:, :, lo:hi].reshape(frames, hi - lo)

    def layer_one(f, total, own_total):
        lo, hi = edges[f], min(edges[f + 1], feat)
        if lo >= hi:
            return total, own_total
        part = weight_cols(lo, hi)
        one = dot(part, frame_cols(lo, hi), ((1,), (1,)))
        two = dot(own[:, lo:hi], part, ((1,), (1,)))
        return (one, two) if total is None else (total + one, own_total + two)

    total, own_total = None, None

    def forwarded(i, f):
        for kind in kinds:
            for way in (0, 1):
                if gather_has(way, kind, i, f):
                    pair(way, kind, i, f, other).wait_recv()
                    repack(came_from(way, kind, i), f)

    for i in range(stages):
        for f in range(CHUNKS):
            for kind in kinds:
                for way in (0, 1):
                    if gather_has(way, kind, i, f):
                        gathered(way, kind, i, f).wait_recv()
                        if kind == 0 and i + 1 < stages:
                            for later in kinds:
                                if gather_has(way, later, i + 1, f):
                                    gather(way, later, i + 1, f).start()
                        pair(way, kind, i, f, side).start()
            if i == 0:
                if f == 0:
                    own_pair(other).wait_recv()
                repack(chip, f)
            else:
                forwarded(i - 1, f)
            if i == stages - 1 and f > 0:
                forwarded(i, f - 1)
                total, own_total = layer_one(f - 1, total, own_total)
        if i == max(0, stages - 2):
            frames_on()
    forwarded(stages - 1, CHUNKS - 1)
    total, own_total = layer_one(CHUNKS - 1, total, own_total)

    second = weight_cols(feat, width)
    second_turned = second.astype(F32).T.astype(BF16)

    def narrow(first):
        act = jnp.maximum(first, 0.0)
        late = dot(act.astype(BF16), second, ((1,), (1,)))
        act = jnp.maximum(late, 0.0) + act
        return dot(head_bf, act.astype(BF16), ((1,), (1,)))

    own_net = narrow(own_total)
    own_out[...] = own_net[:32]
    boot = dot(column(own_net[acts : acts + 1], 8), to_frames, precision=lax.Precision.HIGHEST)[:1]

    act_one = jnp.maximum(total, 0.0)
    one_bf = act_one.astype(BF16)
    pre_two = dot(second, one_bf)
    two_bf = (jnp.maximum(pre_two, 0.0) + act_one).astype(BF16)
    net = dot(small, two_bf)
    out_grad = trace_gradient(net, boot, flat[0:1], flat[1:2], flat[2:3], flat[3:4], acts, steps).astype(BF16)

    head_grad = dot(out_grad, two_bf, ((1,), (1,)))
    half_units = units // 2
    for k in (0, 1):
        head_part[k] = head_grad[:, k * half_units : (k + 1) * half_units].astype(BF16)
    hpair = remote(head_part.at[other], head_from, hpair_send, hpair_recv, sibling)
    hpair.start()

    g_two = dot(head_turned[:, :32], out_grad)
    gp_two = jnp.where(pre_two > 0, g_two, 0.0).astype(BF16)
    g_one = g_two + dot(second_turned, gp_two)
    gp_one = jnp.where(total > 0, g_one, 0.0).astype(BF16)

    hpair.wait_recv()
    head_all[chip] = (head_part[side].astype(F32) + head_from[...].astype(F32)).astype(BF16)

    def head_has(way, kind, i):
        return kind == 1 or i < stages - 1 or way == 0

    def head_ring(way, kind, i):
        block = head_all.at[chip_at(-sign[way] * 2 * i)]
        at = (way, kind, i)
        return remote(block, block, hring_send.at[at], hring_recv.at[at], target[kind][way])

    def head_come(way, kind, i):
        block = head_all.at[came_from(way, kind, i)]
        at = (way, kind, i)
        return remote(block, block, hring_send.at[at], hring_recv.at[at], target[kind][way])

    def head_step(i):
        for way in (0, 1):
            if head_has(way, 0, i):
                head_come(way, 0, i).wait_recv()
                if i + 1 < stages:
                    for later in kinds:
                        if head_has(way, later, i + 1):
                            head_ring(way, later, i + 1).start()

    for kind in kinds:
        for way in (0, 1):
            if head_has(way, kind, 0):
                head_ring(way, kind, 0).start()

    def swap(f):
        return remote(
            for_sibling.at[:, :, cols(f)], from_sibling.at[:, :, cols(f)], half_send.at[f], half_recv.at[f], sibling
        )

    first_side = side == 0
    for f in range(CHUNKS):
        lo, hi = edges[f], edges[f + 1]
        parts = []
        if lo < feat:
            parts.append(dot(gp_one, frame_cols(lo, min(hi, feat))))
        if hi > feat:
            parts.append(dot(gp_two, one_bf, ((1,), (1,))))
        grad = parts[0] if len(parts) == 1 else jnp.concatenate(parts, 1)
        grad = grad.reshape(chips, 2, shard, hi - lo)
        for_sibling[:, :, lo:hi] = jnp.where(first_side, grad[:, 1], grad[:, 0]).astype(BF16)
        swap(f).start()
        mine[:, :, lo:hi] = jnp.where(first_side, grad[:, 0], grad[:, 1])

    def reduce_has(way, kind, i, f):
        return kind == 1 or i > 0 or (f < half) == (way == 0)

    def reduce_to(way, kind, i, f):
        at = (way, kind, i)
        return remote(
            sums_out.at[(*at, slice(None), cols(f))], sums_in.at[(*at, slice(None), cols(f))],
            reduce_send.at[(*at, f)], reduce_recv.at[(*at, f)], target[kind][way],
        )

    def arrived(way, i, f, term):
        for kind in kinds:
            if reduce_has(way, kind, i, f):
                reduce_to(way, kind, i, f).wait_recv()
                term = term + sums_in[way, kind, i, :, cols(f)].astype(F32)
        return term

    def reduce_step(way, i, f):
        for kind in kinds:
            if reduce_has(way, kind, i, f):
                term = mine[chip_at(sign[way] * (far - 2 * i - kind)), :, cols(f)]
                if kind == 0 and i > 0:
                    term = arrived(way, i - 1, f, term)
                sums_out[way, kind, i, :, cols(f)] = term.astype(BF16)
                reduce_to(way, kind, i, f).start()

    for f in range(CHUNKS):
        swap(f).wait_recv()
        lo, hi = edges[f], edges[f + 1]
        mine[:, :, lo:hi] = mine[:, :, lo:hi] + from_sibling[:, :, lo:hi].astype(F32)
        for way in (0, 1):
            reduce_step(way, 0, f)

    def answers_y(i, at):
        return remote(
            played_out.at[:, y_to[i]], played_mid.at[:, at], played_send.at[0, i], played_recv.at[0, i], y_peer[i]
        )

    def answers_x(i, at):
        return remote(
            played_mid.at[x_to[i]], played_in.at[at], played_send.at[1, i], played_recv.at[1, i], x_peer[i]
        )

    def play():
        for i in range(agent_y - 1):
            frames_y(i, y_from[i]).wait_recv()
        came = frames_in[...].astype(F32).reshape(agents * SLOTS, feat).astype(BF16)
        act = jnp.maximum(dot(came, weight_cols(0, feat), ((1,), (1,))), 0.0)
        late = dot(act.astype(BF16), second, ((1,), (1,)))
        act = jnp.maximum(late, 0.0) + act
        answers = dot(act.astype(BF16), head_bf, ((1,), (1,)))
        played_out[...] = answers.reshape(agent_x, agent_y, SLOTS, PAD).astype(BF16)
        for i in range(agent_y - 1):
            answers_y(i, ay).start()
        played_mid[:, ay] = played_out[:, ay]

    def answers_on():
        for i in range(agent_y - 1):
            answers_y(i, y_from[i]).wait_recv()
        for i in range(agent_x - 1):
            answers_x(i, ax).start()
        played_in[ax] = played_mid[ax]

    if stages == 1:
        play()
        answers_on()
    for i in range(1, stages):
        head_step(i - 1)
        for f in range(CHUNKS):
            for way in (0, 1):
                reduce_step(way, i, f)
        if i == max(1, stages - 3):
            play()
        if i == max(1, stages - 2):
            answers_on()

    head_step(stages - 1)
    for i in range(stages):
        for way in (0, 1):
            head_come(way, 1, i).wait_recv()
    head_final[side] = jnp.sum(head_all[...].astype(F32), 0)
    hlast = remote(head_final.at[side], head_final.at[side], hlast_send, hlast_recv, sibling)
    hlast.start()

    for i in range(agent_x - 1):
        answers_x(i, x_from[i]).wait_recv()
    back = played_in[...].astype(F32).reshape(agents * SLOTS, PAD).T.astype(BF16)
    opp_out[...] = dot(back, placed)[:32].astype(BF16)

    for f in range(CHUNKS):
        total = mine[chip, :, cols(f)]
        for way in (0, 1):
            total = arrived(way, stages - 1, f, total)
        grad_out[:, cols(f)] = total

    remote(head_final.at[other], head_final.at[other], hlast_send, hlast_recv, sibling).wait_recv()
    head_out[...] = head_final[...]

    for i in range(stages):
        for kind in kinds:
            for way in (0, 1):
                for f in range(CHUNKS):
                    if gather_has(way, kind, i, f):
                        gather(way, kind, i, f).wait_send()
                        pair(way, kind, i, f, side).wait_send()
                    if reduce_has(way, kind, i, f):
                        reduce_to(way, kind, i, f).wait_send()
                if head_has(way, kind, i):
                    head_ring(way, kind, i).wait_send()
    own_pair(side).wait_send()
    hpair.wait_send()
    hlast.wait_send()
    for f in range(CHUNKS):
        swap(f).wait_send()
    for i in range(agent_x - 1):
        frames_x(i, ax).wait_send()
        answers_x(i, ax).wait_send()
    for i in range(agent_y - 1):
        frames_y(i, ay).wait_send()
        answers_y(i, ay).wait_send()


def adam_step(master, moment, second, grad, rate):
    moment = beta_first * moment + (1.0 - beta_first) * grad
    second = beta_second * second + (1.0 - beta_second) * grad * grad
    master = master - rate * moment / (jnp.sqrt(second) + adam_eps)
    return (master, moment, second)


def finish_kernel(
    head_rows, rate, grad, head_grad, own_net, opp_net, core, core_mom, core_vel, head, head_mom, head_vel,
    own_out, opp_out, new_core, new_mom, new_vel, new_head, new_head_mom, new_head_vel,
):
    by = rate[0]
    new_core[0], new_mom[0], new_vel[0] = adam_step(core[0], core_mom[0], core_vel[0], grad[...], by)
    for i in range(head_rows):
        row = jnp.concatenate([head_grad[0, i : i + 1], head_grad[1, i : i + 1]], 1)
        new_head[i], new_head_mom[i], new_head_vel[i] = adam_step(head[i], head_mom[i], head_vel[i], row, by)
    for i in range(head_rows - 1):
        own_out[i] = own_net[i : i + 1]
    opp_out[0] = opp_net[0 : head_rows - 1]


def per_device(
    learn_obs, own_obs, opp_obs, opponent, actions, done, rewards, behaviour,
    core_master, core_mom, core_vel, head_master, head_mom, head_vel, rates,
):
    _, envs, steps, feat = learn_obs.shape
    _, shard, width = core_master.shape
    _, head_rows, units = head_master.shape
    agents, dp = lax.axis_size("agent"), lax.axis_size("dp")
    chips = dp // 2
    far = chips // 2
    stages = far // 2
    agent_y = 4 if agents % 4 == 0 else agents
    sizes = (agents, chips, shard, envs, steps, feat, units, head_rows, agent_y)
    vmem, dma = pltpu.VMEM, pltpu.SemaphoreType.DMA
    anywhere = pl.BlockSpec(memory_space=pl.ANY)
    in_vmem = pl.BlockSpec(memory_space=vmem)
    head_rows_first = [a.swapaxes(0, 1) for a in (head_master, head_mom, head_vel)]
    grad, head_grad, own_net, opp_net = pl.pallas_call(
        functools.partial(step_kernel, sizes),
        out_shape=(
            vmem((shard, width), F32),
            vmem((2, 32, units // 2), F32),
            vmem((32, envs), F32),
            vmem((32, envs), BF16),
        ),
        in_specs=[anywhere] * 10,
        out_specs=(in_vmem,) * 4,
        scratch_shapes=[
            vmem((envs, steps, feat), BF16),
            vmem((envs, feat), BF16),
            vmem((envs, feat), BF16),
            vmem((1, envs), jnp.int32),
            vmem((steps, envs), jnp.int32),
            vmem((steps, envs), jnp.int32),
            vmem((steps, envs), F32),
            vmem((steps, envs), F32),
            vmem((shard, width), F32),
            vmem((head_rows, 1, units), F32),
            vmem((chips, 2, shard, width), BF16),
            vmem((chips, 2 * shard, width), BF16),
            vmem((chips, shard, width), F32),
            vmem((chips, shard, width), BF16),
            vmem((chips, shard, width), BF16),
            vmem((2, 2, stages, shard, width), BF16),
            vmem((2, 2, stages, shard, width), BF16),
            vmem((agents // agent_y, agent_y, SLOTS, feat), BF16),
            vmem((agents // agent_y, agent_y, SLOTS, feat), BF16),
            vmem((agents // agent_y, agent_y, SLOTS, feat), BF16),
            vmem((agents // agent_y, agent_y, SLOTS, PAD), BF16),
            vmem((agents // agent_y, agent_y, SLOTS, PAD), BF16),
            vmem((agents // agent_y, agent_y, SLOTS, PAD), BF16),
            vmem((PAD, units), F32),
            vmem((2, 32, units // 2), BF16),
            vmem((32, units // 2), BF16),
            vmem((chips, 32, units // 2), BF16),
            vmem((2, 32, units // 2), F32),
            dma((10,)),
            dma((2, 2, stages, CHUNKS)),
            dma((2, 2, stages, CHUNKS)),
            dma((2, 2, stages, CHUNKS)),
            dma((2, 2, stages, CHUNKS)),
            dma,
            dma,
            dma((2, agent_y)),
            dma((2, agent_y)),
            dma((2, agent_y)),
            dma((2, agent_y)),
            dma((2, 2, stages, CHUNKS)),
            dma((2, 2, stages, CHUNKS)),
            dma((CHUNKS,)),
            dma((CHUNKS,)),
            dma((2, 2, stages)),
            dma((2, 2, stages)),
            dma,
            dma,
            dma,
            dma,
        ],
        compiler_params=pltpu.CompilerParams(
            collective_id=0, has_side_effects=True, vmem_limit_bytes=56 * 2**20
        ),
    )(
        learn_obs, own_obs, opp_obs, turned(opponent), turned(actions), turned(done), turned(rewards), turned(behaviour),
        core_master, head_rows_first[0],
    )
    own_logits, opp_logits, *new = pl.pallas_call(
        functools.partial(finish_kernel, head_rows),
        out_shape=(
            jax.ShapeDtypeStruct((head_rows - 1, 1, envs), F32),
            jax.ShapeDtypeStruct((1, head_rows - 1, envs), BF16),
            *[jax.ShapeDtypeStruct((1, shard, width), F32)] * 3,
            *[jax.ShapeDtypeStruct((head_rows, 1, units), F32)] * 3,
        ),
        in_specs=[pl.BlockSpec(memory_space=pltpu.SMEM)] + [in_vmem] * 10,
        out_specs=(in_vmem,) * 8,
        compiler_params=pltpu.CompilerParams(vmem_limit_bytes=8 * 2**20),
    )(rates, grad, head_grad, own_net, opp_net, core_master, core_mom, core_vel, *head_rows_first)
    return (
        own_logits.transpose(1, 2, 0),
        turned(opp_logits),
        *new[:3],
        *[a.swapaxes(0, 1) for a in new[3:]],
    )


def solution(mesh):
    rows, whole = P("agent", "dp"), P("agent")
    return jax.shard_map(
        per_device,
        mesh=mesh,
        in_specs=(rows,) * 11 + (whole,) * 4,
        out_specs=(rows,) * 5 + (whole,) * 3,
        check_vma=False,
    )
```

```python
import functools

import jax
import jax.numpy as jnp
from jax import lax
from jax.experimental import pallas as pl
from jax.experimental.pallas import tpu as pltpu
from jax.sharding import PartitionSpec as P

MESH = pl.DeviceIdType.MESH
F32 = jnp.float32
BF16 = jnp.bfloat16
SLOTS = 8
PAD = 128
CHUNKS = 3

gamma_rate = 0.99
baseline_cost = 0.5
entropy_cost = 0.05
beta_first = 0.9
beta_second = 0.99
adam_eps = 1e-08


def dot(left, right, dims=((1,), (0,)), precision=None):
    return lax.dot_general(left, right, (dims, ((), ())), precision=precision, preferred_element_type=F32)


def bounds(total, parts, unit=128):
    units = -(-total // unit)
    return [min(total, unit * (units * i // parts)) for i in range(parts + 1)]


def turned(x):
    return x.swapaxes(1, 2)


def column(row_vector, sublanes):
    return jnp.broadcast_to(row_vector, (sublanes, row_vector.shape[1]))


def trace_gradient(out, boot, actions, done, rewards, behaviour, actions_total, steps):
    rows, frames = out.shape
    scale = 1.0 / steps
    row = lax.broadcasted_iota(jnp.int32, (rows, frames), 0)
    time = lax.broadcasted_iota(jnp.int32, (8, frames), 1) % steps
    is_logit = row < actions_total
    values = column(out[actions_total : actions_total + 1, :], 8)
    total = jnp.sum(jnp.where(is_logit, jnp.exp(out), 0.0), 0, keepdims=True)
    logp = out - jnp.log(total)
    probs = jnp.where(is_logit, jnp.exp(logp), 0.0)
    chosen = (row.astype(F32) == actions).astype(F32)
    logp_act = jnp.sum(jnp.where(is_logit, logp, 0.0) * chosen, 0, keepdims=True)
    entropy = -jnp.sum(probs * jnp.where(is_logit, logp, 0.0), 0, keepdims=True)
    ratio = column(jnp.minimum(1.0, jnp.exp(logp_act - behaviour)), 8)
    discount = column(gamma_rate * (1.0 - done), 8)
    rewards, boot = column(rewards, 8), column(boot, 8)
    last = time == steps - 1

    def later(x, by):
        return pltpu.roll(x, frames - by, 1)

    next_values = jnp.where(last, boot, later(values, 1))
    corr = ratio * (rewards + discount * next_values - values)
    factor = discount * ratio
    by = 1
    while by < steps:
        inside = time < steps - by
        corr, factor = (
            corr + factor * jnp.where(inside, later(corr, by), 0.0),
            factor * jnp.where(inside, later(factor, by), 0.0),
        )
        by *= 2
    targets = values + corr
    next_targets = jnp.where(last, boot, later(targets, 1))
    advantage = ratio * (rewards + discount * next_targets - values)
    grad_logits = scale * (
        -advantage[:1] * (chosen - probs) + entropy_cost * probs * (logp + entropy)
    )
    grad_value = scale * (-baseline_cost * (targets - values))[:1]
    return jnp.where(is_logit, grad_logits, jnp.where(row == actions_total, grad_value, 0.0))


def step_kernel(
    sizes,
    learn_hbm, own_hbm, opp_hbm, opponent_hbm, actions_hbm, done_hbm, rewards_hbm, behaviour_hbm, core_hbm, head_hbm,
    grad_out, head_out, own_out, opp_out,
    x, own, opp, opponent, actions, done, rewards, behaviour, core, head,
    shards, weights, mine, for_sibling, from_sibling, sums_out, sums_in, frames_out, frames_mid, frames_in,
    played_out, played_mid, played_in, heads, head_part, head_from, head_all, head_final,
    load_sem, gather_send, gather_recv, pair_send, pair_recv, own_send, own_recv,
    frame_send, frame_recv, played_send, played_recv, reduce_send, reduce_recv,
    half_send, half_recv, hring_send, hring_recv, hpair_send, hpair_recv, hlast_send, hlast_recv,
):
    (agents, chips, shard, envs, steps, feat, units, head_rows, agent_y) = sizes
    frames = envs * steps
    width = feat + units
    acts = head_rows - 1
    edges = bounds(width, CHUNKS)
    far = chips // 2
    half = CHUNKS // 2
    stages = far // 2
    agent, dp = lax.axis_index("agent"), lax.axis_index("dp")
    chip, side = dp // 2, dp % 2
    other = 1 - side
    agent_x = agents // agent_y
    ax, ay = agent // agent_y, agent % agent_y

    def chip_at(offset):
        return lax.rem(chip + (offset + 2 * chips), chips)

    sibling = (agent, 2 * chip + other)
    sign = [1, -1]
    next_one = [(agent, 2 * chip_at(k) + side) for k in sign]
    next_two = [(agent, 2 * chip_at(2 * k) + side) for k in sign]
    target = [next_two, next_one]
    x_to = [lax.rem(ax + i, agent_x) for i in range(1, agent_x)]
    x_from = [lax.rem(ax + agent_x - i, agent_x) for i in range(1, agent_x)]
    y_to = [lax.rem(ay + i, agent_y) for i in range(1, agent_y)]
    y_from = [lax.rem(ay + agent_y - i, agent_y) for i in range(1, agent_y)]
    x_peer = [(k * agent_y + ay, dp) for k in x_to]
    y_peer = [(ax * agent_y + k, dp) for k in y_to]

    barrier = pltpu.get_barrier_semaphore()
    peers = [*next_two, *next_one, *x_peer, *y_peer, sibling]
    for peer in peers:
        pl.semaphore_signal(barrier, inc=1, device_id=peer, device_id_type=MESH)

    loads = [
        pltpu.make_async_copy(src, dst, load_sem.at[i])
        for i, (src, dst) in enumerate((
            (core_hbm.at[0], core), (head_hbm, head), (opponent_hbm.at[0], opponent), (opp_hbm.at[0], opp),
            (learn_hbm.at[0], x), (own_hbm.at[0], own), (actions_hbm.at[0], actions), (done_hbm.at[0], done),
            (rewards_hbm.at[0], rewards), (behaviour_hbm.at[0], behaviour),
        ))
    ]
    for load in loads:
        load.start()

    def cols(f):
        return pl.ds(edges[f], edges[f + 1] - edges[f])

    def remote(src, dst, send, recv, to):
        return pltpu.make_async_remote_copy(
            src_ref=src, dst_ref=dst, send_sem=send, recv_sem=recv, device_id=to, device_id_type=MESH
        )

    kinds = (0, 1)

    def gather_has(way, kind, i, f):
        return kind == 1 or i < stages - 1 or (f < half) == (way == 0)

    def gather(way, kind, i, f):
        block = shards.at[chip_at(-sign[way] * 2 * i), side, :, cols(f)]
        at = (way, kind, i, f)
        return remote(block, block, gather_send.at[at], gather_recv.at[at], target[kind][way])

    def came_from(way, kind, i):
        return chip_at(-sign[way] * (2 * i + 2 - kind))

    def gathered(way, kind, i, f):
        block = shards.at[came_from(way, kind, i), side, :, cols(f)]
        at = (way, kind, i, f)
        return remote(block, block, gather_send.at[at], gather_recv.at[at], target[kind][way])

    def pair(way, kind, i, f, which):
        block = shards.at[came_from(way, kind, i), which, :, cols(f)]
        at = (way, kind, i, f)
        return remote(block, block, pair_send.at[at], pair_recv.at[at], sibling)

    def own_pair(which):
        block = shards.at[chip, which]
        return remote(block, block, own_send, own_recv, sibling)

    loads[0].wait()
    shards[chip, side] = core[...].astype(BF16)

    pl.semaphore_wait(barrier, len(peers))
    for kind in kinds:
        for f in range(CHUNKS):
            for way in (0, 1):
                if gather_has(way, kind, 0, f):
                    gather(way, kind, 0, f).start()
    own_pair(side).start()

    loads[2].wait()
    ids = opponent[...]
    agent_row = lax.broadcasted_iota(jnp.int32, (PAD, envs), 0)
    member = (ids == agent_row).astype(F32)
    before = (
        lax.broadcasted_iota(jnp.int32, (envs, envs), 0) < lax.broadcasted_iota(jnp.int32, (envs, envs), 1)
    ).astype(BF16)
    ranks = jnp.sum(dot(member.astype(BF16), before) * member, 0, keepdims=True)
    position = ids * SLOTS + ranks.astype(jnp.int32)
    slot_row = lax.broadcasted_iota(jnp.int32, (agents * SLOTS, envs), 0)
    placed = (position == slot_row).astype(BF16)
    loads[3].wait()
    frames_out[...] = dot(placed, opp[...]).reshape(agent_x, agent_y, SLOTS, feat).astype(BF16)

    def frames_x(i, at):
        return remote(frames_out.at[x_to[i]], frames_mid.at[at], frame_send.at[0, i], frame_recv.at[0, i], x_peer[i])

    def frames_y(i, at):
        return remote(
            frames_mid.at[:, y_to[i]], frames_in.at[:, at], frame_send.at[1, i], frame_recv.at[1, i], y_peer[i]
        )

    for i in range(agent_x - 1):
        frames_x(i, ax).start()
    frames_mid[ax] = frames_out[ax]

    def frames_on():
        for i in range(agent_x - 1):
            frames_x(i, x_from[i]).wait_recv()
        for i in range(agent_y - 1):
            frames_y(i, ay).start()
        frames_in[:, ay] = frames_mid[:, ay]


    loads[1].wait()
    heads[...] = jnp.zeros_like(heads)
    for i in range(head_rows):
        heads[i : i + 1, :] = head[i]
    head_bf = heads[...].astype(BF16)
    head_turned = heads[...].T.astype(BF16)
    small = head_bf[:32]

    for load in loads[6:]:
        load.wait()
    stacked = jnp.concatenate(
        [actions[...].astype(F32), done[...].astype(F32), rewards[...], behaviour[...]], 0
    )
    env_lane = lax.broadcasted_iota(jnp.int32, (envs, frames), 1)
    to_frames = (env_lane // steps == lax.broadcasted_iota(jnp.int32, (envs, frames), 0)).astype(F32)
    spread = dot(stacked, to_frames, precision=lax.Precision.HIGHEST).reshape(4, steps, frames)
    same_step = (
        lax.broadcasted_iota(jnp.int32, (steps, frames), 1) % steps
        == lax.broadcasted_iota(jnp.int32, (steps, frames), 0)
    )
    flat = jnp.sum(jnp.where(same_step[None], spread, 0.0), 1)

    loads[4].wait()
    loads[5].wait()

    def repack(at, f):
        pair_of = [shards[at, k, :, cols(f)].astype(F32) for k in (0, 1)]
        weights[at, :, cols(f)] = jnp.concatenate(pair_of, 0).astype(BF16)

    def weight_cols(lo, hi):
        return weights[:, :, lo:hi].reshape(units, hi - lo)

    def frame_cols(lo, hi):
        return x[:, :, lo:hi].reshape(frames, hi - lo)

    def layer_one(f, total, own_total):
        lo, hi = edges[f], min(edges[f + 1], feat)
        if lo >= hi:
            return total, own_total
        part = weight_cols(lo, hi)
        one = dot(part, frame_cols(lo, hi), ((1,), (1,)))
        two = dot(own[:, lo:hi], part, ((1,), (1,)))
        return (one, two) if total is None else (total + one, own_total + two)

    total, own_total = None, None

    def forwarded(i, f):
        for kind in kinds:
            for way in (0, 1):
                if gather_has(way, kind, i, f):
                    pair(way, kind, i, f, other).wait_recv()
                    repack(came_from(way, kind, i), f)

    for i in range(stages):
        for f in range(CHUNKS):
            for kind in kinds:
                for way in (0, 1):
                    if gather_has(way, kind, i, f):
                        gathered(way, kind, i, f).wait_recv()
                        if kind == 0 and i + 1 < stages:
                            for later in kinds:
                                if gather_has(way, later, i + 1, f):
                                    gather(way, later, i + 1, f).start()
                        pair(way, kind, i, f, side).start()
            if i == 0:
                if f == 0:
                    own_pair(other).wait_recv()
                repack(chip, f)
            else:
                forwarded(i - 1, f)
            if i == stages - 1 and f > 0:
                forwarded(i, f - 1)
                total, own_total = layer_one(f - 1, total, own_total)
        if i == max(0, stages - 2):
            frames_on()
    forwarded(stages - 1, CHUNKS - 1)
    total, own_total = layer_one(CHUNKS - 1, total, own_total)

    second = weight_cols(feat, width)
    second_turned = second.astype(F32).T.astype(BF16)

    def narrow(first):
        act = jnp.maximum(first, 0.0)
        late = dot(act.astype(BF16), second, ((1,), (1,)))
        act = jnp.maximum(late, 0.0) + act
        return dot(head_bf, act.astype(BF16), ((1,), (1,)))

    own_net = narrow(own_total)
    own_out[...] = own_net[:32]
    boot = dot(column(own_net[acts : acts + 1], 8), to_frames, precision=lax.Precision.HIGHEST)[:1]

    act_one = jnp.maximum(total, 0.0)
    one_bf = act_one.astype(BF16)
    pre_two = dot(second, one_bf)
    two_bf = (jnp.maximum(pre_two, 0.0) + act_one).astype(BF16)
    net = dot(small, two_bf)
    out_grad = trace_gradient(net, boot, flat[0:1], flat[1:2], flat[2:3], flat[3:4], acts, steps).astype(BF16)

    head_grad = dot(out_grad, two_bf, ((1,), (1,)))
    half_units = units // 2
    for k in (0, 1):
        head_part[k] = head_grad[:, k * half_units : (k + 1) * half_units].astype(BF16)
    hpair = remote(head_part.at[other], head_from, hpair_send, hpair_recv, sibling)
    hpair.start()

    g_two = dot(head_turned[:, :32], out_grad)
    gp_two = jnp.where(pre_two > 0, g_two, 0.0).astype(BF16)
    g_one = g_two + dot(second_turned, gp_two)
    gp_one = jnp.where(total > 0, g_one, 0.0).astype(BF16)

    hpair.wait_recv()
    head_all[chip] = (head_part[side].astype(F32) + head_from[...].astype(F32)).astype(BF16)

    def head_has(way, kind, i):
        return kind == 1 or i < stages - 1 or way == 0

    def head_ring(way, kind, i):
        block = head_all.at[chip_at(-sign[way] * 2 * i)]
        at = (way, kind, i)
        return remote(block, block, hring_send.at[at], hring_recv.at[at], target[kind][way])

    def head_come(way, kind, i):
        block = head_all.at[came_from(way, kind, i)]
        at = (way, kind, i)
        return remote(block, block, hring_send.at[at], hring_recv.at[at], target[kind][way])

    def head_step(i):
        for way in (0, 1):
            if head_has(way, 0, i):
                head_come(way, 0, i).wait_recv()
                if i + 1 < stages:
                    for later in kinds:
                        if head_has(way, later, i + 1):
                            head_ring(way, later, i + 1).start()

    for kind in kinds:
        for way in (0, 1):
            if head_has(way, kind, 0):
                head_ring(way, kind, 0).start()

    def swap(f):
        return remote(
            for_sibling.at[:, :, cols(f)], from_sibling.at[:, :, cols(f)], half_send.at[f], half_recv.at[f], sibling
        )

    def reduce_has(way, kind, i, f):
        return kind == 1 or i > 0 or (f < half) == (way == 0)

    def reduce_to(way, kind, i, f):
        at = (way, kind, i)
        return remote(
            sums_out.at[(*at, slice(None), cols(f))], sums_in.at[(*at, slice(None), cols(f))],
            reduce_send.at[(*at, f)], reduce_recv.at[(*at, f)], target[kind][way],
        )

    def arrived(way, i, f, term):
        for kind in kinds:
            if reduce_has(way, kind, i, f):
                reduce_to(way, kind, i, f).wait_recv()
                term = term + sums_in[way, kind, i, :, cols(f)].astype(F32)
        return term

    def reduce_step(way, i, f):
        for kind in kinds:
            if reduce_has(way, kind, i, f):
                term = mine[chip_at(sign[way] * (far - 2 * i - kind)), :, cols(f)]
                if kind == 0 and i > 0:
                    term = arrived(way, i - 1, f, term)
                sums_out[way, kind, i, :, cols(f)] = term.astype(BF16)
                reduce_to(way, kind, i, f).start()

    def first_stage(f):
        swap(f).wait_recv()
        lo, hi = edges[f], edges[f + 1]
        mine[:, :, lo:hi] = mine[:, :, lo:hi] + from_sibling[:, :, lo:hi].astype(F32)
        for way in (0, 1):
            reduce_step(way, 0, f)

    first_side = side == 0
    for f in range(CHUNKS):
        lo, hi = edges[f], edges[f + 1]
        parts = []
        if lo < feat:
            parts.append(dot(gp_one, frame_cols(lo, min(hi, feat))))
        if hi > feat:
            parts.append(dot(gp_two, one_bf, ((1,), (1,))))
        grad = parts[0] if len(parts) == 1 else jnp.concatenate(parts, 1)
        grad = grad.reshape(chips, 2, shard, hi - lo)
        for_sibling[:, :, lo:hi] = jnp.where(first_side, grad[:, 1], grad[:, 0]).astype(BF16)
        swap(f).start()
        mine[:, :, lo:hi] = jnp.where(first_side, grad[:, 0], grad[:, 1])
        if f > 0:
            first_stage(f - 1)
    first_stage(CHUNKS - 1)

    def answers_y(i, at):
        return remote(
            played_out.at[:, y_to[i]], played_mid.at[:, at], played_send.at[0, i], played_recv.at[0, i], y_peer[i]
        )

    def answers_x(i, at):
        return remote(
            played_mid.at[x_to[i]], played_in.at[at], played_send.at[1, i], played_recv.at[1, i], x_peer[i]
        )

    def play():
        for i in range(agent_y - 1):
            frames_y(i, y_from[i]).wait_recv()
        came = frames_in[...].astype(F32).reshape(agents * SLOTS, feat).astype(BF16)
        act = jnp.maximum(dot(came, weight_cols(0, feat), ((1,), (1,))), 0.0)
        late = dot(act.astype(BF16), second, ((1,), (1,)))
        act = jnp.maximum(late, 0.0) + act
        answers = dot(act.astype(BF16), head_bf, ((1,), (1,)))
        played_out[...] = answers.reshape(agent_x, agent_y, SLOTS, PAD).astype(BF16)
        for i in range(agent_y - 1):
            answers_y(i, ay).start()
        played_mid[:, ay] = played_out[:, ay]

    def answers_on():
        for i in range(agent_y - 1):
            answers_y(i, y_from[i]).wait_recv()
        for i in range(agent_x - 1):
            answers_x(i, ax).start()
        played_in[ax] = played_mid[ax]

    if stages == 1:
        play()
        answers_on()
    for i in range(1, stages):
        head_step(i - 1)
        for f in range(CHUNKS):
            for way in (0, 1):
                reduce_step(way, i, f)
        if i == max(1, stages - 3):
            play()
        if i == max(1, stages - 2):
            answers_on()

    head_step(stages - 1)
    for i in range(stages):
        for way in (0, 1):
            head_come(way, 1, i).wait_recv()
    head_final[side] = jnp.sum(head_all[...].astype(F32), 0)
    hlast = remote(head_final.at[side], head_final.at[side], hlast_send, hlast_recv, sibling)
    hlast.start()

    for i in range(agent_x - 1):
        answers_x(i, x_from[i]).wait_recv()
    back = played_in[...].astype(F32).reshape(agents * SLOTS, PAD).T.astype(BF16)
    opp_out[...] = dot(back, placed)[:32].astype(BF16)

    for f in range(CHUNKS):
        total = mine[chip, :, cols(f)]
        for way in (0, 1):
            total = arrived(way, stages - 1, f, total)
        grad_out[:, cols(f)] = total

    remote(head_final.at[other], head_final.at[other], hlast_send, hlast_recv, sibling).wait_recv()
    head_out[...] = head_final[...]

    for i in range(stages):
        for kind in kinds:
            for way in (0, 1):
                for f in range(CHUNKS):
                    if gather_has(way, kind, i, f):
                        gather(way, kind, i, f).wait_send()
                        pair(way, kind, i, f, side).wait_send()
                    if reduce_has(way, kind, i, f):
                        reduce_to(way, kind, i, f).wait_send()
                if head_has(way, kind, i):
                    head_ring(way, kind, i).wait_send()
    own_pair(side).wait_send()
    hpair.wait_send()
    hlast.wait_send()
    for f in range(CHUNKS):
        swap(f).wait_send()
    for i in range(agent_x - 1):
        frames_x(i, ax).wait_send()
        answers_x(i, ax).wait_send()
    for i in range(agent_y - 1):
        frames_y(i, ay).wait_send()
        answers_y(i, ay).wait_send()


def adam_step(master, moment, second, grad, rate):
    moment = beta_first * moment + (1.0 - beta_first) * grad
    second = beta_second * second + (1.0 - beta_second) * grad * grad
    master = master - rate * moment / (jnp.sqrt(second) + adam_eps)
    return (master, moment, second)


def finish_kernel(
    head_rows, rate, grad, head_grad, own_net, opp_net, core, core_mom, core_vel, head, head_mom, head_vel,
    own_out, opp_out, new_core, new_mom, new_vel, new_head, new_head_mom, new_head_vel,
):
    by = rate[0]
    new_core[0], new_mom[0], new_vel[0] = adam_step(core[0], core_mom[0], core_vel[0], grad[...], by)
    for i in range(head_rows):
        row = jnp.concatenate([head_grad[0, i : i + 1], head_grad[1, i : i + 1]], 1)
        new_head[i], new_head_mom[i], new_head_vel[i] = adam_step(head[i], head_mom[i], head_vel[i], row, by)
    for i in range(head_rows - 1):
        own_out[i] = own_net[i : i + 1]
    opp_out[0] = opp_net[0 : head_rows - 1]


def per_device(
    learn_obs, own_obs, opp_obs, opponent, actions, done, rewards, behaviour,
    core_master, core_mom, core_vel, head_master, head_mom, head_vel, rates,
):
    _, envs, steps, feat = learn_obs.shape
    _, shard, width = core_master.shape
    _, head_rows, units = head_master.shape
    agents, dp = lax.axis_size("agent"), lax.axis_size("dp")
    chips = dp // 2
    far = chips // 2
    stages = far // 2
    agent_y = 4 if agents % 4 == 0 else agents
    sizes = (agents, chips, shard, envs, steps, feat, units, head_rows, agent_y)
    vmem, dma = pltpu.VMEM, pltpu.SemaphoreType.DMA
    anywhere = pl.BlockSpec(memory_space=pl.ANY)
    in_vmem = pl.BlockSpec(memory_space=vmem)
    head_rows_first = [a.swapaxes(0, 1) for a in (head_master, head_mom, head_vel)]
    grad, head_grad, own_net, opp_net = pl.pallas_call(
        functools.partial(step_kernel, sizes),
        out_shape=(
            vmem((shard, width), F32),
            vmem((2, 32, units // 2), F32),
            vmem((32, envs), F32),
            vmem((32, envs), BF16),
        ),
        in_specs=[anywhere] * 10,
        out_specs=(in_vmem,) * 4,
        scratch_shapes=[
            vmem((envs, steps, feat), BF16),
            vmem((envs, feat), BF16),
            vmem((envs, feat), BF16),
            vmem((1, envs), jnp.int32),
            vmem((steps, envs), jnp.int32),
            vmem((steps, envs), jnp.int32),
            vmem((steps, envs), F32),
            vmem((steps, envs), F32),
            vmem((shard, width), F32),
            vmem((head_rows, 1, units), F32),
            vmem((chips, 2, shard, width), BF16),
            vmem((chips, 2 * shard, width), BF16),
            vmem((chips, shard, width), F32),
            vmem((chips, shard, width), BF16),
            vmem((chips, shard, width), BF16),
            vmem((2, 2, stages, shard, width), BF16),
            vmem((2, 2, stages, shard, width), BF16),
            vmem((agents // agent_y, agent_y, SLOTS, feat), BF16),
            vmem((agents // agent_y, agent_y, SLOTS, feat), BF16),
            vmem((agents // agent_y, agent_y, SLOTS, feat), BF16),
            vmem((agents // agent_y, agent_y, SLOTS, PAD), BF16),
            vmem((agents // agent_y, agent_y, SLOTS, PAD), BF16),
            vmem((agents // agent_y, agent_y, SLOTS, PAD), BF16),
            vmem((PAD, units), F32),
            vmem((2, 32, units // 2), BF16),
            vmem((32, units // 2), BF16),
            vmem((chips, 32, units // 2), BF16),
            vmem((2, 32, units // 2), F32),
            dma((10,)),
            dma((2, 2, stages, CHUNKS)),
            dma((2, 2, stages, CHUNKS)),
            dma((2, 2, stages, CHUNKS)),
            dma((2, 2, stages, CHUNKS)),
            dma,
            dma,
            dma((2, agent_y)),
            dma((2, agent_y)),
            dma((2, agent_y)),
            dma((2, agent_y)),
            dma((2, 2, stages, CHUNKS)),
            dma((2, 2, stages, CHUNKS)),
            dma((CHUNKS,)),
            dma((CHUNKS,)),
            dma((2, 2, stages)),
            dma((2, 2, stages)),
            dma,
            dma,
            dma,
            dma,
        ],
        compiler_params=pltpu.CompilerParams(
            collective_id=0, has_side_effects=True, vmem_limit_bytes=56 * 2**20
        ),
    )(
        learn_obs, own_obs, opp_obs, turned(opponent), turned(actions), turned(done), turned(rewards), turned(behaviour),
        core_master, head_rows_first[0],
    )
    own_logits, opp_logits, *new = pl.pallas_call(
        functools.partial(finish_kernel, head_rows),
        out_shape=(
            jax.ShapeDtypeStruct((head_rows - 1, 1, envs), F32),
            jax.ShapeDtypeStruct((1, head_rows - 1, envs), BF16),
            *[jax.ShapeDtypeStruct((1, shard, width), F32)] * 3,
            *[jax.ShapeDtypeStruct((head_rows, 1, units), F32)] * 3,
        ),
        in_specs=[pl.BlockSpec(memory_space=pltpu.SMEM)] + [in_vmem] * 10,
        out_specs=(in_vmem,) * 8,
        compiler_params=pltpu.CompilerParams(vmem_limit_bytes=8 * 2**20),
    )(rates, grad, head_grad, own_net, opp_net, core_master, core_mom, core_vel, *head_rows_first)
    return (
        own_logits.transpose(1, 2, 0),
        turned(opp_logits),
        *new[:3],
        *[a.swapaxes(0, 1) for a in new[3:]],
    )


def solution(mesh):
    rows, whole = P("agent", "dp"), P("agent")
    return jax.shard_map(
        per_device,
        mesh=mesh,
        in_specs=(rows,) * 11 + (whole,) * 4,
        out_specs=(rows,) * 5 + (whole,) * 3,
        check_vma=False,
    )
```
